256 devices in a mesh: member: 4 (over y_hi, core), grid: 64 (over x, y_lo, z).
Axes of the slice: x: 4, y: 4 (y_hi: 2, y_lo: 2; y = y_hi * 2 + y_lo), z: 8, core: 2. Of those that a mesh axis runs over, the one named last changes fastest.
Arguments:
- ensemble: bfloat16 [8, 4096, 1024], P('member', 'grid'), may hold values from -6 to 6
- target_field: bfloat16 [4096, 1024], P('grid'), may hold values from -6 to 6
- weight_in: bfloat16 [1024, 3072], P('grid')
- weight_out: bfloat16 [1024, 1024], P('grid'), may hold values from -0.1875 to 0.1875
- window_start: int32 [4096], P('grid'), may hold values from 0 to 4095, as said below
- window_end: int32 [4096], P('grid'), may hold values from 1 to 4096, as said below
Outputs:
- grad_input: bfloat16 [8, 4096, 1024], P('member', 'grid')
- grad_weight_in: float32 [1024, 3072], P('grid')
- grad_weight_out: float32 [1024, 1024], P('grid')
The draws below stay inside these ranges and needn't reach their ends.
Inputs may be any that keep to these rules, and one draw needn't show every extreme that they name: window_start[i] <= i < window_end[i] and i - 64 <= window_start[i]; on every index of grid but the first some points have window_start[i] = i - 64. window_end[i] <= i + 65; on every index of grid but the last some points have window_end[i] = i + 65.
All inputs are finite; a program needn't handle non-finite values.
Results may differ from the reference program's by a relative error of at most 0.019.
Values may be sent and summed in bfloat16 or wider, within the bound.
A program may use at most 128 MiB of HBM per device.

```python
import math
import jax
import jax.numpy as jnp
from jax import lax

CHANNELS = 1024
HEADS = 16
MEMBERS = 8
PTS_DEV = 64
POINTS = 4096
REACH = 64


def draw_weight_in(key, part):
    key = jax.random.fold_in(key, 11)
    base = jax.random.normal(key, (CHANNELS, 3 * CHANNELS), jnp.float32) * CHANNELS ** (-0.5)
    return base.astype(jnp.bfloat16)


def window_sides(key):
    index = jnp.arange(POINTS, dtype=jnp.int32)
    below = jax.random.randint(jax.random.fold_in(key, 101), (POINTS,), 0, REACH + 1, jnp.int32)
    above = jax.random.randint(jax.random.fold_in(key, 102), (POINTS,), 0, REACH + 1, jnp.int32)
    widest = index % 16 == 3
    below = jnp.where(widest, REACH, below)
    above = jnp.where(widest, REACH, above)
    return (index, below, above)


def draw_window_start(key, part):
    index, below, above = window_sides(key)
    return jnp.maximum(index - below, 0).astype(jnp.int32)


def draw_window_end(key, part):
    index, below, above = window_sides(key)
    return jnp.minimum(index + 1 + above, POINTS).astype(jnp.int32)


def block_levels(rng, dims, shards, smallest, top_value):
    def one(position, parts):
        steps = jax.random.uniform(jax.random.fold_in(jax.random.fold_in(rng, 6), position), (parts,), jnp.float32, smallest / len(shards), top_value / len(shards))
        return jnp.repeat(jnp.exp(steps), dims[position] // parts).reshape((-1,) + (1,) * (len(dims) - position - 1))

    loudness = one(*shards[0])
    for cut in shards[1:]:
        loudness = loudness * one(*cut)
    return loudness


def scatter_about(own_key, shape, deviation, most, cuts=(), kind=jnp.bfloat16):
    entries = deviation * jax.random.normal(own_key, shape, jnp.float32)
    if cuts:
        entries = entries * block_levels(own_key, shape, cuts, -0.22, 0.18)
    return jnp.clip(entries, -most, most).astype(kind)


def setup_inputs(seed: int = 0) -> dict:
    splits = jax.random.split(jax.random.key(seed), 7)
    return {
        "ensemble": scatter_about(splits[0], (MEMBERS, POINTS, CHANNELS), 1.0, 6.0, ((0, 4), (1, 64))),
        "target_field": scatter_about(splits[1], (POINTS, CHANNELS), 1.0, 6.0, ((0, 64),)),
        "weight_in": draw_weight_in(jax.random.fold_in(splits[6], 71), 0),
        "weight_out": scatter_about(splits[3], (CHANNELS, CHANNELS), CHANNELS ** -0.5, 0.1875, ((0, 64),)),
        "window_start": draw_window_start(jax.random.fold_in(splits[6], 71), 0),
        "window_end": draw_window_end(jax.random.fold_in(splits[6], 71), 0),
    }


norm_eps = 1e-05
smooth_width = 0.1
fair_alpha = 0.95
masked_score = -1e+30

def norm_rows(values):
    wide = values.astype(jnp.float32)
    center = wide - lax.optimization_barrier(jnp.mean(wide, axis=-1, keepdims=True))
    inverse = lax.rsqrt(lax.optimization_barrier(jnp.mean(center * center, axis=-1, keepdims=True)) + norm_eps)
    return (center * inverse, inverse)

def slope(delta):
    return delta / jnp.sqrt(delta * delta + smooth_width * smooth_width)

def crps_slope(members_all, target, own):
    count = members_all.shape[0]
    spread = jnp.zeros(own.shape, jnp.float32)
    for member in range(count):
        spread = spread + slope(own - members_all[member][None])
    fair = (1.0 - fair_alpha) / count
    return slope(own - target[None]) - (1.0 - fair) / (count - 1) * spread

def split_heads(block_rows, width):
    blocks, span, channels = block_rows.shape
    return block_rows.astype(jnp.float32).reshape(blocks, span, HEADS, channels // HEADS)

def attend(queries, keyvals, starts, ends, offsets):
    blocks, rows, width = queries.shape
    span = keyvals.shape[1]
    scale = 1.0 / math.sqrt(width // HEADS)
    query_heads = split_heads(queries, width)
    key_heads = split_heads(keyvals[..., :width], width)
    value_heads = split_heads(keyvals[..., width:], width)
    scores = jnp.einsum('bphd,bkhd->bhpk', query_heads, key_heads, precision=lax.Precision.HIGHEST) * scale
    positions = offsets[:, None] + jnp.arange(span, dtype=jnp.int32)[None]
    valid = (positions[:, None, :] >= starts[:, :, None]) & (positions[:, None, :] < ends[:, :, None])
    scores = jnp.where(valid[:, None], scores, masked_score)
    highest = lax.optimization_barrier(jnp.max(scores, axis=-1, keepdims=True))
    raised = jnp.exp(scores - highest)
    weights = raised / lax.optimization_barrier(jnp.sum(raised, axis=-1, keepdims=True))
    rounded = weights.astype(jnp.bfloat16)
    mixed = jnp.einsum('bhpk,bkhd->bphd', rounded.astype(jnp.float32), value_heads, precision=lax.Precision.HIGHEST)
    return (mixed.reshape(blocks, rows, width).astype(jnp.bfloat16), weights, rounded)

def attend_back(queries, keyvals, mixed, weights, rounded, grad_mixed):
    blocks, rows, width = queries.shape
    span = keyvals.shape[1]
    scale = 1.0 / math.sqrt(width // HEADS)
    query_heads = split_heads(queries, width)
    key_heads = split_heads(keyvals[..., :width], width)
    value_heads = split_heads(keyvals[..., width:], width)
    grad_heads = split_heads(grad_mixed, width)
    grad_weights = jnp.einsum('bphd,bkhd->bhpk', grad_heads, value_heads, precision=lax.Precision.HIGHEST)
    grad_values = jnp.einsum('bhpk,bphd->bkhd', rounded.astype(jnp.float32), grad_heads, precision=lax.Precision.HIGHEST)
    inner = (grad_heads * split_heads(mixed, width)).sum(-1)
    inner = jnp.transpose(inner, (0, 2, 1))[..., None]
    grad_scores = (weights * (grad_weights - inner)).astype(jnp.bfloat16).astype(jnp.float32)
    grad_queries = jnp.einsum('bhpk,bkhd->bphd', grad_scores, key_heads, precision=lax.Precision.HIGHEST) * scale
    grad_keys = jnp.einsum('bhpk,bphd->bkhd', grad_scores, query_heads, precision=lax.Precision.HIGHEST) * scale
    grad_keyvals = jnp.concatenate([grad_keys.reshape(blocks, span, width), grad_values.reshape(blocks, span, width)], axis=-1)
    return (grad_queries.reshape(blocks, rows, width), grad_keyvals)

def block_view(queries, keyvals, window_start, window_end):
    blocks = POINTS // PTS_DEV
    padded = jnp.pad(keyvals, ((REACH, REACH), (0, 0)))
    index = jnp.arange(blocks, dtype=jnp.int32)[:, None] * PTS_DEV + jnp.arange(PTS_DEV + 2 * REACH, dtype=jnp.int32)[None]
    extended = padded[index]
    offsets = jnp.arange(blocks, dtype=jnp.int32) * PTS_DEV - REACH
    return (queries.reshape(blocks, PTS_DEV, CHANNELS), extended, window_start.reshape(blocks, PTS_DEV), window_end.reshape(blocks, PTS_DEV), offsets)

def reference(ensemble, target_field, weight_in, weight_out, window_start, window_end):
    normed, inverse = norm_rows(ensemble)
    normed_b = normed.astype(jnp.bfloat16)
    flat_normed = normed_b.reshape(-1, CHANNELS)
    projected = jnp.dot(flat_normed, weight_in, preferred_element_type=jnp.float32).astype(jnp.bfloat16)
    projected = projected.reshape(MEMBERS, POINTS, 3 * CHANNELS)
    queries = projected[..., :CHANNELS]
    keyvals = projected[..., CHANNELS:]

    def member_forward(operands):
        view = block_view(operands[0], operands[1], window_start, window_end)
        return attend(*view)[0].reshape(POINTS, CHANNELS)
    attended = lax.map(member_forward, (queries, keyvals))
    flat_attended = attended.reshape(-1, CHANNELS)
    output = ensemble.reshape(-1, CHANNELS).astype(jnp.float32) + jnp.dot(flat_attended, weight_out, preferred_element_type=jnp.float32)
    output = output.astype(jnp.bfloat16).reshape(MEMBERS, POINTS, CHANNELS).astype(jnp.float32)
    cotangent = crps_slope(output, target_field.astype(jnp.float32), output).astype(jnp.bfloat16)
    flat_cotangent = cotangent.reshape(-1, CHANNELS)
    grad_attended = jnp.dot(flat_cotangent, weight_out.T, preferred_element_type=jnp.float32).astype(jnp.bfloat16)
    grad_attended = grad_attended.reshape(MEMBERS, POINTS, CHANNELS)

    def member_backward(operands):
        view = block_view(operands[0], operands[1], window_start, window_end)
        mixed, weights, rounded = attend(*view)
        blocks = POINTS // PTS_DEV
        grad_queries, grad_ext = attend_back(view[0], view[1], mixed, weights, rounded, operands[2].reshape(blocks, PTS_DEV, CHANNELS))
        middle = grad_ext[:, REACH:REACH + PTS_DEV]
        lower = grad_ext[:, :REACH]
        upper = grad_ext[:, REACH + PTS_DEV:]
        middle = middle.at[:-1, PTS_DEV - REACH:].add(lower[1:])
        middle = middle.at[1:, :REACH].add(upper[:-1])
        return (grad_queries.reshape(POINTS, CHANNELS), middle.reshape(POINTS, 2 * CHANNELS))
    grad_queries, grad_keyvals = lax.map(member_backward, (queries, keyvals, grad_attended))
    grad_projected = jnp.concatenate([grad_queries, grad_keyvals], axis=-1).astype(jnp.bfloat16)
    flat_grad = grad_projected.reshape(-1, 3 * CHANNELS)
    grad_normed = jnp.dot(flat_grad, weight_in.T, preferred_element_type=jnp.float32).reshape(MEMBERS, POINTS, CHANNELS)
    first = lax.optimization_barrier(jnp.mean(grad_normed, axis=-1, keepdims=True))
    second = lax.optimization_barrier(jnp.mean(grad_normed * normed, axis=-1, keepdims=True))
    grad_input = (cotangent.astype(jnp.float32) + inverse * (grad_normed - first - normed * second)).astype(jnp.bfloat16)
    factor = 1.0 / math.sqrt(MEMBERS * POINTS)
    grad_weight_in = jnp.dot(flat_normed.T, flat_grad, preferred_element_type=jnp.float32) * factor
    grad_weight_out = jnp.dot(flat_attended.T, flat_cotangent, preferred_element_type=jnp.float32) * factor
    return (grad_input, grad_weight_in, grad_weight_out)
```

```python
import functools
import math

import jax
import jax.numpy as jnp
from jax import lax
from jax.experimental import pallas as pl
from jax.experimental.pallas import tpu as pltpu
from jax.sharding import PartitionSpec as P

HEADS = 16
REACH = 64
MESH = pl.DeviceIdType.MESH


class Place:
    def __init__(self):
        g = lax.axis_index("grid")
        m = lax.axis_index("member")
        self.x, self.yl, self.z = g // 16, (g // 8) % 2, g % 8
        self.yh, self.c = m // 2, m % 2

    def dev(self, x, yl, z, yh, c):
        return (yh * 2 + c, (x * 2 + yl) * 8 + z)

    def zoff(self, s):
        return self.dev(self.x, self.yl, (self.z + s + 8) % 8, self.yh, self.c)

    def xoff(self, s):
        return self.dev((self.x + s + 4) % 4, self.yl, self.z, self.yh, self.c)

    def yoff(self, s):
        y = (2 * self.yh + self.yl + s + 4) % 4
        return self.dev(self.x, y % 2, self.z, y // 2, self.c)

    def sibling(self):
        return self.dev(self.x, self.yl, self.z, self.yh, 1 - self.c)

    def greet(self, partners):
        barrier = pltpu.get_barrier_semaphore()
        for partner in partners:
            pl.semaphore_signal(barrier, 1, device_id=partner, device_id_type=MESH)
        pl.semaphore_wait(barrier, len(partners))


def remote(src, dst, send, recv, device):
    copy = pltpu.make_async_remote_copy(
        src_ref=src, dst_ref=dst, send_sem=send, recv_sem=recv, device_id=device, device_id_type=MESH
    )
    copy.start()
    return copy


def await_bytes(ref, sem):
    pltpu.make_async_copy(ref, ref, sem).wait()


def rows_at(start, count, unit=16):
    return pl.ds(pl.multiple_of(start, unit), count)


def gather_rows(place, buf, cols, z_send, z_recv, x_send, x_recv, y_send, y_recv):
    x, yl, z = place.x, place.yl, place.z
    half = cols // 2
    block = lambda xs: yl * 512 + ((x + xs + 4) % 4) * 128
    shard = lambda s: buf.at[rows_at(block(0) + ((z + s + 8) % 8) * 16, 16)]

    def pass_on(s):
        ref = shard(s)
        remote(ref, ref, x_send.at[0], x_recv.at[0], place.xoff(1))
        remote(ref, ref, x_send.at[1], x_recv.at[1], place.xoff(-1))
        side = 0 if s in (0, 1, 2, 3) else 1
        remote(ref, ref, y_send.at[side], y_recv.at[side, 0], place.yoff(1 if side == 0 else -1))

    z_copies = []
    for step in range(4):
        if step:
            await_bytes(shard(-step), z_recv.at[0, step - 1])
            await_bytes(shard(step), z_recv.at[1, step - 1])
        for way, sign in ((0, 1), (1, -1)):
            ref = shard(-sign * step)
            if step == 3:
                ref = ref.at[:, pl.ds(way * half, half)]
            z_copies.append(
                remote(ref, ref, z_send.at[way, step], z_recv.at[way, step], place.zoff(sign))
            )
        if step == 0:
            pass_on(0)
        else:
            pass_on(-step)
            pass_on(step)
    for way in range(2):
        await_bytes(shard(4).at[:, pl.ds(way * half, half)], z_recv.at[way, 3])
    pass_on(4)

    def y_block(index, xs):
        for side, sign in ((0, 1), (1, -1)):
            ref = buf.at[rows_at(block(xs) + side * 64, 64)]
            remote(ref, ref, y_send.at[side], y_recv.at[side, index], place.yoff(sign))

    for way, sign in ((0, 1), (1, -1)):
        await_bytes(buf.at[rows_at(block(-sign), 128)], x_recv.at[way])
        ref = buf.at[rows_at(block(-sign) + way * 64, 64)]
        remote(ref, ref, x_send.at[way], x_recv.at[2 + way], place.xoff(sign))
    y_block(1, -1)
    y_block(2, 1)
    for way in range(2):
        await_bytes(buf.at[rows_at(block(2) + way * 64, 64)], x_recv.at[2 + way])
    y_block(3, 2)
    for copy in z_copies:
        copy.wait_send()

    def finish():
        for side in range(2):
            for index in range(4):
                await_bytes(buf.at[pl.ds(0, 64)], y_recv.at[side, index])
            await_bytes(buf.at[pl.ds(0, 192)], x_send.at[side])
            await_bytes(buf.at[pl.ds(0, 256)], y_send.at[side])

    return finish


def gather_kernel(w_ref, out_ref, buf, z_send, z_recv, x_send, x_recv, y_send, y_recv, d_send, d_recv, out_sem):
    place = Place()
    c = place.c
    cols = buf.shape[2]
    mine = buf.at[0]
    own = place.yl * 512 + place.x * 128 + place.z * 16
    mine[rows_at(own, 16), :] = w_ref[:, pl.ds(pl.multiple_of(c * cols, cols), cols)]
    place.greet(
        [place.zoff(1), place.zoff(-1), place.xoff(1), place.xoff(-1), place.yoff(1), place.yoff(-1), place.sibling()]
    )
    gather_rows(place, mine, cols, z_send, z_recv, x_send, x_recv, y_send, y_recv)()
    copy = remote(mine, buf.at[1], d_send, d_recv, place.sibling())
    outs = []

    def put(slot, lane):
        for yl in range(2):
            for x in range(4):
                index = yl * 4 + x
                out = pltpu.make_async_copy(
                    buf.at[slot, pl.ds(index * 128, 128)],
                    out_ref.at[pl.ds((x * 2 + yl) * 128, 128), pl.ds(pl.multiple_of(lane * cols, cols), cols)],
                    out_sem.at[slot, index],
                )
                out.start()
                outs.append(out)

    put(0, c)
    copy.wait()
    put(1, 1 - c)
    for out in outs:
        out.wait()


def gather_weights(shard):
    rows, width = shard.shape
    total = rows * lax.axis_size("grid")
    cols = width // 2
    dma = pltpu.SemaphoreType.DMA
    return pl.pallas_call(
        gather_kernel,
        name="k_gather",
        out_shape=jax.ShapeDtypeStruct((total, width), shard.dtype),
        in_specs=[pl.BlockSpec(memory_space=pltpu.VMEM)],
        out_specs=pl.BlockSpec(memory_space=pl.ANY),
        scratch_shapes=[
            pltpu.VMEM((2, total, cols), shard.dtype),
            dma((2, 4)), dma((2, 4)), dma((2,)), dma((4,)), dma((2,)), dma((2, 4)),
            dma, dma, dma((2, 8)),
        ],
        compiler_params=pltpu.CompilerParams(
            collective_id=1, has_side_effects=True, vmem_limit_bytes=40 << 20
        ),
    )(shard)


def add_rows(dst, src, start, count):
    dst[rows_at(start, count), :] = (
        dst[rows_at(start, count), :].astype(jnp.float32) + src.astype(jnp.float32)
    ).astype(dst.dtype)


def scatter_rows(place, part, y_stage, x_stage, x_last, z_stage, y_send, y_recv, x_send, x_recv, z_send, z_recv):
    x, yl, z = place.x, place.yl, place.z
    block = lambda xs: ((x + xs + 4) % 4) * 128
    mine, other = yl * 512, (1 - yl) * 512
    order = (2, 1, -1, 0)
    for index, xs in enumerate(order):
        for side, sign in ((0, 1), (1, -1)):
            start = block(xs) + side * 64
            remote(
                part.at[rows_at(other + start, 64)], y_stage.at[rows_at(start, 64)],
                y_send.at[side], y_recv.at[side, index], place.yoff(sign),
            )

    def take_y(index, xs):
        start = block(xs)
        for side in range(2):
            await_bytes(y_stage.at[rows_at(start + side * 64, 64)], y_recv.at[side, index])
        for sub in range(4):
            add_rows(part, y_stage[rows_at(start + sub * 32, 32), :], mine + start + sub * 32, 32)

    copies = []
    take_y(0, 2)
    for way, sign in ((0, 1), (1, -1)):
        ref = part.at[rows_at(mine + block(2) + way * 64, 64)]
        copies.append(
            remote(ref, x_stage.at[pl.ds(way * 64, 64)], x_send.at[0, way], x_recv.at[0, way], place.xoff(sign))
        )
    for way, sign in ((0, 1), (1, -1)):
        take_y(1 + way, sign)
        copies[way].wait_recv()
        for sub in range(2):
            add_rows(part, x_stage[pl.ds(way * 64 + sub * 32, 32), :], mine + block(sign) + way * 64 + sub * 32, 32)
        copies.append(
            remote(
                part.at[rows_at(mine + block(sign), 128)], x_last.at[way],
                x_send.at[1, way], x_recv.at[1, way], place.xoff(sign),
            )
        )
    take_y(3, 0)
    for way in range(2):
        copies[2 + way].wait_recv()
    for sub in range(4):
        both = x_last[0, pl.ds(sub * 32, 32), :].astype(jnp.float32) + x_last[1, pl.ds(sub * 32, 32), :].astype(
            jnp.float32
        )
        add_rows(part, both, mine + block(0) + sub * 32, 32)
    row = lambda s: rows_at(mine + block(0) + ((z + s) % 8) * 16, 16)
    z_copies = [
        remote(part.at[row(s)], z_stage.at[s], z_send.at[s], z_recv.at[s], place.zoff(s)) for s in (4, 3, 5, 2, 6, 1, 7)
    ]
    for copy in z_copies:
        copy.wait_recv()
    total = part[row(0), :].astype(jnp.float32)
    for s in range(1, 8):
        total = total + z_stage[s].astype(jnp.float32)
    for copy in copies + z_copies:
        copy.wait_send()
    for side in range(2):
        await_bytes(part.at[pl.ds(0, 256)], y_send.at[side])
    return total


def scatter_kernel(
    factor, term_ref, out_ref, part, from_sibling, y_stage, x_stage, x_last, z_stage, pair, shared,
    y_send, y_recv, x_send, x_recv, z_send, z_recv, d_send, d_recv, in_sem,
):
    place = Place()
    c = place.c
    cols = part.shape[1]
    lane = lambda k: pl.ds(pl.multiple_of(k * cols, cols), cols)
    ins = []
    for yl in range(2):
        for x in range(4):
            index = yl * 4 + x
            copy = pltpu.make_async_copy(
                term_ref.at[pl.ds((x * 2 + yl) * 128, 128), lane(c)],
                part.at[pl.ds(index * 128, 128)],
                in_sem.at[index],
            )
            copy.start()
            ins.append(copy)
    place.greet(
        [place.zoff(s) for s in range(1, 8)]
        + [place.xoff(1), place.xoff(-1), place.yoff(1), place.yoff(-1), place.yoff(2), place.sibling()]
    )
    gives = []
    for yl in range(2):
        for x in range(4):
            index = yl * 4 + x
            gives.append(
                remote(
                    term_ref.at[pl.ds((x * 2 + yl) * 128, 128), lane(1 - c)],
                    from_sibling.at[pl.ds(index * 128, 128)],
                    d_send.at[index], d_recv.at[index], place.sibling(),
                )
            )
    for copy in ins:
        copy.wait()
    for copy in gives:
        copy.wait()

    @pl.loop(0, 32)
    def _(step):
        add_rows(part, from_sibling[rows_at(step * 32, 32), :], step * 32, 32)

    total = scatter_rows(place, part, y_stage, x_stage, x_last, z_stage, y_send, y_recv, x_send, x_recv, z_send, z_recv)
    pair[0] = total.astype(pair.dtype)
    copy = remote(pair.at[0], pair.at[1], d_send.at[8], d_recv.at[8], place.yoff(2))
    copy.wait()
    shared[0] = (pair[0].astype(jnp.float32) + pair[1].astype(jnp.float32)) * factor
    copy = remote(shared.at[0], shared.at[1], d_send.at[9], d_recv.at[9], place.sibling())
    copy.wait()
    out_ref[:, lane(c)] = shared[0]
    out_ref[:, lane(1 - c)] = shared[1]


def scatter_gradients(term, factor):
    total, width = term.shape
    cols = width // 2
    dma = pltpu.SemaphoreType.DMA
    kind = term.dtype
    return pl.pallas_call(
        functools.partial(scatter_kernel, factor),
        name="k_scatter",
        out_shape=jax.ShapeDtypeStruct((16, width), jnp.float32),
        in_specs=[pl.BlockSpec(memory_space=pl.ANY)],
        out_specs=pl.BlockSpec(memory_space=pltpu.VMEM),
        scratch_shapes=[
            pltpu.VMEM((total, cols), kind),
            pltpu.VMEM((total, cols), kind),
            pltpu.VMEM((512, cols), kind),
            pltpu.VMEM((128, cols), kind),
            pltpu.VMEM((2, 128, cols), kind),
            pltpu.VMEM((8, 16, cols), kind),
            pltpu.VMEM((2, 16, cols), kind),
            pltpu.VMEM((2, 16, cols), jnp.float32),
            dma((2,)), dma((2, 4)), dma((2, 2)), dma((2, 2)), dma((8,)), dma((8,)),
            dma((10,)), dma((10,)), dma((8,)),
        ],
        compiler_params=pltpu.CompilerParams(
            collective_id=2, has_side_effects=True, vmem_limit_bytes=48 << 20
        ),
    )(term)


norm_eps = 1e-05
smooth_width = 0.1
fair_alpha = 0.95
masked_score = -1e30


def extended_2(cells, sides, width):
    for axis, dim in sides:
        count = lax.axis_size(axis)
        ends = count - 1
        head = lax.slice_in_dim(cells, 0, width, axis=dim)
        tail = lax.slice_in_dim(cells, cells.shape[dim] - width, cells.shape[dim], axis=dim)
        cells = jnp.concatenate(
            [
                lax.ppermute(tail, axis, [(i, (i + 1) % count) for i in range(ends)]),
                cells,
                lax.ppermute(head, axis, [((i + 1) % count, i) for i in range(ends)]),
            ],
            axis=dim,
        )
    return cells


def passed_along(block, axis, distance):
    devices = range(lax.axis_size(axis))
    route = [(i - distance, i) for i in devices if i - distance in devices]
    return lax.ppermute(block, axis, route)


def norm_rows(values):
    wide = values.astype(jnp.float32)
    center = wide - jnp.mean(wide, axis=-1, keepdims=True)
    inverse = lax.rsqrt(jnp.mean(center * center, axis=-1, keepdims=True) + norm_eps)
    return (center * inverse, inverse)


def slope(delta):
    return delta / jnp.sqrt(delta * delta + smooth_width * smooth_width)


def crps_slope(members_all, target, own):
    count = members_all.shape[0]
    spread = jnp.zeros(own.shape, jnp.float32)
    for member in range(count):
        spread = spread + slope(own - members_all[member][None])
    fair = (1.0 - fair_alpha) / count
    return slope(own - target[None]) - (1.0 - fair) / (count - 1) * spread


def split_heads(block_rows):
    blocks, span, channels = block_rows.shape
    return block_rows.reshape(blocks, span, HEADS, channels // HEADS)


def attend(queries, keyvals, starts, ends, offsets):
    blocks, rows, width = queries.shape
    span = keyvals.shape[1]
    scale = 1.0 / math.sqrt(width // HEADS)
    query_heads = split_heads(queries)
    key_heads = split_heads(keyvals[..., :width])
    value_heads = split_heads(keyvals[..., width:])
    scores = (
        jnp.einsum("bphd,bkhd->bhpk", query_heads, key_heads, preferred_element_type=jnp.float32)
        * scale
    )
    positions = offsets[:, None] + jnp.arange(span, dtype=jnp.int32)[None]
    valid = (positions[:, None, :] >= starts[:, :, None]) & (
        positions[:, None, :] < ends[:, :, None]
    )
    scores = jnp.where(valid[:, None], scores, masked_score)
    highest = jnp.max(scores, axis=-1, keepdims=True)
    raised = jnp.exp(scores - highest)
    weights = raised / jnp.sum(raised, axis=-1, keepdims=True)
    rounded = weights.astype(jnp.bfloat16)
    mixed = jnp.einsum("bhpk,bkhd->bphd", rounded, value_heads, preferred_element_type=jnp.float32)
    return (mixed.reshape(blocks, rows, width).astype(jnp.bfloat16), weights, rounded)


def attend_back(queries, keyvals, mixed, weights, rounded, grad_mixed):
    blocks, rows, width = queries.shape
    span = keyvals.shape[1]
    scale = 1.0 / math.sqrt(width // HEADS)
    query_heads = split_heads(queries)
    key_heads = split_heads(keyvals[..., :width])
    value_heads = split_heads(keyvals[..., width:])
    grad_heads = split_heads(grad_mixed)
    grad_weights = jnp.einsum(
        "bphd,bkhd->bhpk", grad_heads, value_heads, preferred_element_type=jnp.float32
    )
    grad_values = jnp.einsum(
        "bhpk,bphd->bkhd", rounded, grad_heads, preferred_element_type=jnp.float32
    )
    inner = (grad_heads.astype(jnp.float32) * split_heads(mixed).astype(jnp.float32)).sum(-1)
    inner = jnp.transpose(inner, (0, 2, 1))[..., None]
    grad_scores = (weights * (grad_weights - inner)).astype(jnp.bfloat16)
    grad_queries = (
        jnp.einsum("bhpk,bkhd->bphd", grad_scores, key_heads, preferred_element_type=jnp.float32)
        * scale
    )
    grad_keys = (
        jnp.einsum("bhpk,bphd->bkhd", grad_scores, query_heads, preferred_element_type=jnp.float32)
        * scale
    )
    grad_keyvals = jnp.concatenate(
        [grad_keys.reshape(blocks, span, width), grad_values.reshape(blocks, span, width)], axis=-1
    )
    return (grad_queries.reshape(blocks, rows, width), grad_keyvals)


def local(ensemble, target_field, weight_in, weight_out, window_start, window_end):
    mem_dev, points_here, width = ensemble.shape
    full = gather_weights(jnp.concatenate([weight_in, weight_out], axis=1))
    full_in, full_out = full[:, : 3 * width], full[:, 3 * width :]
    normed, inverse = norm_rows(ensemble)
    normed_b = normed.astype(jnp.bfloat16)
    flat_normed = normed_b.reshape(-1, width)
    projected = jnp.dot(flat_normed, full_in, preferred_element_type=jnp.float32).astype(
        jnp.bfloat16
    )
    projected = projected.reshape(mem_dev, points_here, 3 * width)
    queries = projected[..., :width]
    keyvals = projected[..., width:]
    extended = extended_2(keyvals, (("grid", 1),), REACH)
    first_point = lax.axis_index("grid") * points_here - REACH
    offsets = jnp.full((mem_dev,), first_point, jnp.int32)
    starts = jnp.broadcast_to(window_start[None], (mem_dev, points_here))
    ends = jnp.broadcast_to(window_end[None], (mem_dev, points_here))
    attended, weights, rounded = attend(queries, extended, starts, ends, offsets)
    flat_attended = attended.reshape(-1, width)
    output = ensemble.reshape(-1, width).astype(jnp.float32) + jnp.dot(
        flat_attended, full_out, preferred_element_type=jnp.float32
    )
    output = output.astype(jnp.bfloat16).reshape(mem_dev, points_here, width)
    everyone = lax.all_gather(output, "member", axis=0, tiled=True)
    cotangent = crps_slope(
        everyone.astype(jnp.float32), target_field.astype(jnp.float32), output.astype(jnp.float32)
    ).astype(jnp.bfloat16)
    flat_cotangent = cotangent.reshape(-1, width)
    grad_attended = lax.dot_general(
        flat_cotangent, full_out, (((1,), (1,)), ((), ())), preferred_element_type=jnp.float32
    ).astype(jnp.bfloat16)
    grad_attended = grad_attended.reshape(mem_dev, points_here, width)
    grad_queries, grad_ext = attend_back(
        queries, extended, attended, weights, rounded, grad_attended
    )
    middle = grad_ext[:, REACH : REACH + points_here]
    lower = grad_ext[:, :REACH]
    upper = grad_ext[:, REACH + points_here :]
    from_next = passed_along(lower.astype(jnp.bfloat16), "grid", -1).astype(lower.dtype)
    from_prior = passed_along(upper.astype(jnp.bfloat16), "grid", 1).astype(upper.dtype)
    middle = middle.at[:, points_here - REACH :].add(from_next)
    middle = middle.at[:, :REACH].add(from_prior)
    grad_projected = jnp.concatenate([grad_queries, middle], axis=-1).astype(jnp.bfloat16)
    flat_grad = grad_projected.reshape(-1, 3 * width)
    grad_normed = lax.dot_general(
        flat_grad, full_in, (((1,), (1,)), ((), ())), preferred_element_type=jnp.float32
    ).reshape(mem_dev, points_here, width)
    first = jnp.mean(grad_normed, axis=-1, keepdims=True)
    second = jnp.mean(grad_normed * normed, axis=-1, keepdims=True)
    grad_input = (
        cotangent.astype(jnp.float32) + inverse * (grad_normed - first - normed * second)
    ).astype(jnp.bfloat16)
    member_count = lax.axis_size("member")
    grid_count = lax.axis_size("grid")
    term_in = lax.dot_general(
        flat_normed, flat_grad, (((0,), (0,)), ((), ())), preferred_element_type=jnp.float32
    )
    term_out = lax.dot_general(
        flat_attended, flat_cotangent, (((0,), (0,)), ((), ())), preferred_element_type=jnp.float32
    )
    factor = 1.0 / math.sqrt(mem_dev * member_count * points_here * grid_count)
    summed = scatter_gradients(
        jnp.concatenate([term_in, term_out], axis=1).astype(jnp.bfloat16), factor
    )
    grad_weight_in = summed[:, : 3 * width]
    grad_weight_out = summed[:, 3 * width :]
    return (grad_input, grad_weight_in, grad_weight_out)


def solution(mesh):
    in_specs = (
        P("member", "grid", None),
        P("grid", None),
        P("grid", None),
        P("grid", None),
        P("grid"),
        P("grid"),
    )
    out_specs = (P("member", "grid", None), P("grid", None), P("grid", None))
    return jax.shard_map(local, mesh=mesh, in_specs=in_specs, out_specs=out_specs, check_vma=False)
```

```python
import functools
import math

import jax
import jax.numpy as jnp
from jax import lax
from jax.experimental import pallas as pl
from jax.experimental.pallas import tpu as pltpu
from jax.sharding import PartitionSpec as P

MESH = pl.DeviceIdType.MESH


class Place:
    def __init__(self):
        g = lax.axis_index("grid")
        m = lax.axis_index("member")
        self.x, self.yl, self.z = g // 16, (g // 8) % 2, g % 8
        self.yh, self.c = m // 2, m % 2

    def dev(self, x, yl, z, yh, c):
        return (yh * 2 + c, (x * 2 + yl) * 8 + z)

    def zoff(self, s):
        return self.dev(self.x, self.yl, (self.z + s + 8) % 8, self.yh, self.c)

    def xoff(self, s):
        return self.dev((self.x + s + 4) % 4, self.yl, self.z, self.yh, self.c)

    def yoff(self, s):
        y = (2 * self.yh + self.yl + s + 4) % 4
        return self.dev(self.x, y % 2, self.z, y // 2, self.c)

    def sibling(self):
        return self.dev(self.x, self.yl, self.z, self.yh, 1 - self.c)

    def goff(self, s):
        g = ((self.x * 2 + self.yl) * 8 + self.z + s + 64) % 64
        return (self.yh * 2 + self.c, g)

    def greet(self, partners):
        barrier = pltpu.get_barrier_semaphore()
        for partner in partners:
            pl.semaphore_signal(barrier, 1, device_id=partner, device_id_type=MESH)
        pl.semaphore_wait(barrier, len(partners))


def remote(src, dst, send, recv, device):
    copy = pltpu.make_async_remote_copy(
        src_ref=src, dst_ref=dst, send_sem=send, recv_sem=recv, device_id=device, device_id_type=MESH
    )
    copy.start()
    return copy


def await_bytes(ref, sem):
    pltpu.make_async_copy(ref, ref, sem).wait()


def rows_at(start, count, unit=16):
    return pl.ds(pl.multiple_of(start, unit), count)


def lanes(start, count):
    return pl.ds(pl.multiple_of(start, 128), count)


def dot(a, b, dims):
    return lax.dot_general(a, b, (dims, ((), ())), preferred_element_type=jnp.float32)


NN = ((1,), (0,))
NT = ((1,), (1,))
TN = ((0,), (0,))


class Sems:
    def __init__(self, array):
        self.array, self.used = array, 0

    def take(self, count=None):
        start = self.used
        self.used += 1 if count is None else count
        if count is None:
            return self.array.at[start]
        return [self.array.at[start + i] for i in range(count)]

    def run(self, count):
        start = self.used
        self.used += count
        return lambda i: self.array.at[start + i]


class Gather:
    def __init__(self, place, buf, sems):
        self.place, self.buf, self.cols = place, buf, buf.shape[1]
        self.z_send, self.z_recv = [sems.take(4), sems.take(4)], [sems.take(4), sems.take(4)]
        self.x_send, self.x_recv = sems.take(2), sems.take(4)
        self.y_send, self.y_recv = sems.take(2), [sems.take(4), sems.take(4)]
        self.z_copies = []

    def block(self, xs):
        return self.place.yl * 512 + ((self.place.x + xs + 4) % 4) * 128

    def shard(self, s):
        return self.buf.at[rows_at(self.block(0) + ((self.place.z + s + 8) % 8) * 16, 16)]

    def pass_on(self, s):
        ref, place = self.shard(s), self.place
        remote(ref, ref, self.x_send[0], self.x_recv[0], place.xoff(1))
        remote(ref, ref, self.x_send[1], self.x_recv[1], place.xoff(-1))
        side = 0 if s in (0, 1, 2, 3) else 1
        remote(ref, ref, self.y_send[side], self.y_recv[side][0], place.yoff(1 if side == 0 else -1))

    def z_step(self, step):
        half = self.cols // 2
        if 0 < step < 4:
            await_bytes(self.shard(-step), self.z_recv[0][step - 1])
            await_bytes(self.shard(step), self.z_recv[1][step - 1])
        if step == 4:
            for way in range(2):
                await_bytes(self.shard(4).at[:, pl.ds(way * half, half)], self.z_recv[way][3])
            return
        for way, sign in ((0, 1), (1, -1)):
            ref = self.shard(-sign * step)
            if step == 3:
                ref = ref.at[:, pl.ds(way * half, half)]
            self.z_copies.append(
                remote(ref, ref, self.z_send[way][step], self.z_recv[way][step], self.place.zoff(sign))
            )

    def y_block(self, index, xs):
        for side, sign in ((0, 1), (1, -1)):
            ref = self.buf.at[rows_at(self.block(xs) + side * 64, 64)]
            remote(ref, ref, self.y_send[side], self.y_recv[side][index], self.place.yoff(sign))

    def x_one(self):
        for way, sign in ((0, 1), (1, -1)):
            await_bytes(self.buf.at[rows_at(self.block(-sign), 128)], self.x_recv[way])
            ref = self.buf.at[rows_at(self.block(-sign) + way * 64, 64)]
            remote(ref, ref, self.x_send[way], self.x_recv[2 + way], self.place.xoff(sign))
        self.y_block(1, -1)
        self.y_block(2, 1)

    def x_two(self):
        for way in range(2):
            await_bytes(self.buf.at[rows_at(self.block(2) + way * 64, 64)], self.x_recv[2 + way])
        self.y_block(3, 2)

    def finish(self):
        for copy in self.z_copies:
            copy.wait_send()
        for side in range(2):
            for index in range(4):
                await_bytes(self.buf.at[pl.ds(0, 64)], self.y_recv[side][index])
            await_bytes(self.buf.at[pl.ds(0, 192)], self.x_send[side])
            await_bytes(self.buf.at[pl.ds(0, 256)], self.y_send[side])


def add_rows(dst, src, start, count):
    dst[rows_at(start, count), :] = (
        dst[rows_at(start, count), :].astype(jnp.float32) + src.astype(jnp.float32)
    ).astype(dst.dtype)


class Scatter:
    def __init__(self, place, part, y_stage, x_stage, x_last, z_stage, sems):
        self.place, self.part, self.y_stage = place, part, y_stage
        self.x_stage, self.x_last, self.z_stage = x_stage, x_last, z_stage
        self.y_send, self.y_recv = sems.take(2), [sems.take(4), sems.take(4)]
        self.x_send, self.x_recv = sems.take(4), sems.take(4)
        self.z_send, self.z_recv = sems.take(8), sems.take(8)
        self.copies = []
        self.mine, self.other = place.yl * 512, (1 - place.yl) * 512

    def block(self, xs):
        return ((self.place.x + xs + 4) % 4) * 128

    def y_start(self):
        for index, xs in enumerate((2, 1, -1, 0)):
            for side, sign in ((0, 1), (1, -1)):
                start = self.block(xs) + side * 64
                remote(
                    self.part.at[rows_at(self.other + start, 64)], self.y_stage.at[rows_at(start, 64)],
                    self.y_send[side], self.y_recv[side][index], self.place.yoff(sign),
                )

    def take_y(self, index, xs):
        start = self.block(xs)
        for side in range(2):
            await_bytes(self.y_stage.at[rows_at(start + side * 64, 64)], self.y_recv[side][index])
        for sub in range(4):
            add_rows(self.part, self.y_stage[rows_at(start + sub * 32, 32), :], self.mine + start + sub * 32, 32)

    def x_one(self):
        self.take_y(0, 2)
        for way, sign in ((0, 1), (1, -1)):
            ref = self.part.at[rows_at(self.mine + self.block(2) + way * 64, 64)]
            self.copies.append(
                remote(ref, self.x_stage.at[pl.ds(way * 64, 64)], self.x_send[way], self.x_recv[way],
                       self.place.xoff(sign))
            )

    def x_two(self):
        for way, sign in ((0, 1), (1, -1)):
            self.take_y(1 + way, sign)
            self.copies[way].wait_recv()
            for sub in range(2):
                at = way * 64 + sub * 32
                add_rows(self.part, self.x_stage[pl.ds(at, 32), :], self.mine + self.block(sign) + at, 32)
            self.copies.append(
                remote(self.part.at[rows_at(self.mine + self.block(sign), 128)], self.x_last.at[way],
                       self.x_send[2 + way], self.x_recv[2 + way], self.place.xoff(sign))
            )

    def row(self, s):
        return rows_at(self.mine + self.block(0) + ((self.place.z + s) % 8) * 16, 16)

    def z_start(self):
        self.take_y(3, 0)
        for way in range(2):
            self.copies[2 + way].wait_recv()
        for sub in range(4):
            at = pl.ds(sub * 32, 32)
            both = self.x_last[0, at, :].astype(jnp.float32) + self.x_last[1, at, :].astype(jnp.float32)
            add_rows(self.part, both, self.mine + self.block(0) + sub * 32, 32)
        self.z_copies = [
            remote(self.part.at[self.row(s)], self.z_stage.at[s], self.z_send[s], self.z_recv[s], self.place.zoff(s))
            for s in (4, 3, 5, 2, 6, 1, 7)
        ]

    def total(self):
        for copy in self.z_copies:
            copy.wait_recv()
        total = self.part[self.row(0), :].astype(jnp.float32)
        for s in range(1, 8):
            total = total + self.z_stage[s].astype(jnp.float32)
        return total

    def finish(self):
        for copy in self.copies + self.z_copies:
            copy.wait_send()
        for side in range(2):
            await_bytes(self.part.at[pl.ds(0, 256)], self.y_send[side])


SEMS = 232
PAIRS = (0, 2, 1, 3)


def spot(block):
    return (block % 2) * 4 + block // 2


def normed_of(wide):
    center = wide - jnp.mean(wide, axis=-1, keepdims=True)
    inverse = lax.rsqrt(jnp.mean(center * center, axis=-1, keepdims=True) + norm_eps)
    return center * inverse, inverse


def slope(delta):
    return delta * lax.rsqrt(delta * delta + smooth_width * smooth_width)


def head_masks():
    lane = lax.broadcasted_iota(jnp.int32, (64, 256), 1) // 64
    return [(lane == h).astype(jnp.float32) for h in range(4)]


def spread_heads(block, masks):
    wide = block.astype(jnp.float32)
    return jnp.concatenate([(wide * mask).astype(jnp.bfloat16) for mask in masks], axis=0)


def fold_heads(wide, masks):
    total = wide[0:64] * masks[0]
    for h in range(1, 4):
        total = total + wide[h * 64 : (h + 1) * 64] * masks[h]
    return total


def whole_kernel(
    factor, ens_ref, target_ref, win_ref, wout_ref, bounds_ref, gin_ref, gwin_ref, gwout_ref,
    w_in, w_out, ens, nrm, nrm_t, q, kv, acc_q, acc_kv, mask, probs, att, att_t, outs, cot, cot_full,
    ga_send, ga_recv, ga, gp, own_kv, h_send, h_recv, gn, gn_recv,
    part_o, y_o, x_o, l_o, z_o, part_q, y_q, x_q, l_q, z_q, part_k, y_k, x_k, l_k, z_k,
    pair, shared, sem_array,
):
    place = Place()
    sems = Sems(sem_array)
    c, yl = place.c, place.yl
    own = yl * 512 + place.x * 128 + place.z * 16
    bf16, f32 = jnp.bfloat16, jnp.float32
    for sec in range(3):
        for p in range(4):
            w_in[rows_at(own, 16), pl.ds(sec * 512 + p * 128, 128)] = win_ref[
                :, lanes(sec * 1024 + c * 512 + PAIRS[p] * 128, 128)
            ]
    w_out[rows_at(own, 16), :] = wout_ref[:, lanes(c * 512, 512)]
    ens[1, rows_at(c * 128, 128), :] = ens_ref[...]
    place.greet(
        [place.zoff(s) for s in range(1, 8)]
        + [place.xoff(1), place.xoff(-1), place.yoff(1), place.yoff(-1), place.yoff(2), place.sibling()]
        + [place.goff(1), place.goff(-1)]
    )
    gi, go = Gather(place, w_in, sems), Gather(place, w_out, sems)
    gi.z_step(0)
    gi.pass_on(0)
    mine = rows_at(c * 128, 128)
    theirs = rows_at((1 - c) * 128, 128)
    ens_own = remote(ens_ref, ens.at[1, mine], sems.take(), sems.take(), place.sibling())
    for step in (1, 2, 3):
        gi.z_step(step)
        gi.pass_on(-step)
        gi.pass_on(step)
    halo = [
        remote(ens_ref, ens.at[0, mine], sems.take(), sems.take(), place.goff(1)),
        remote(ens_ref, ens.at[2, mine], sems.take(), sems.take(), place.goff(-1)),
    ]
    go.z_step(0)
    gi.z_step(4)
    gi.pass_on(4)

    def norm_block(b):
        @pl.loop(0, 8)
        def _(step):
            rows = rows_at(step * 32, 32)
            normed = normed_of(ens[b, rows, :].astype(f32))[0].astype(bf16)
            for block in range(8):
                nrm[b, rows, pl.ds(spot(block) * 128, 128)] = normed[:, block * 128 : (block + 1) * 128]

    ens_own.wait()
    norm_block(1)
    go.z_step(1)

    @pl.loop(0, 8)
    def _(j):
        nrm_t[rows_at(j * 128, 128), :] = nrm[1, :, lanes(j * 128, 128)].T

    position = place.goff(0)[1] * 64 - 64 + lax.broadcasted_iota(jnp.int32, (192, 256), 0)
    valid = (position >= bounds_ref[0:1, :]) & (position < bounds_ref[1:2, :])
    mask[...] = valid.astype(f32)
    go.z_step(2)
    gi.x_one()
    go.z_step(3)
    for copy in halo:
        copy.wait_recv()
    onward = [
        remote(ens.at[b, mine], ens.at[b, mine], sems.take(), sems.take(), place.sibling()) for b in (0, 2)
    ]
    gi.x_two()
    go.z_step(4)
    for s in (0, -1, 1, -2, 2, -3, 3, 4):
        go.pass_on(s)
    for copy in onward:
        copy.wait()
    for copy in halo:
        copy.wait_send()
    norm_block(0)
    norm_block(2)

    half_one, half_two = lanes(yl * 512, 512), lanes((1 - yl) * 512, 512)

    @pl.loop(0, 4)
    def _(j):
        cols = lanes(512 + j * 256, 256)
        to = lanes(j * 256, 256)
        for b in range(3):
            acc_kv[b, :, to] = dot(nrm[b, :, half_one], w_in[half_one, cols], NN)

    @pl.loop(0, 2)
    def _(j):
        cols = lanes(j * 256, 256)
        acc_q[:, cols] = dot(nrm[1, :, half_one], w_in[half_one, cols], NN)

    go.x_one()
    gi.finish()

    @pl.loop(0, 4)
    def _(j):
        cols = lanes(512 + j * 256, 256)
        to = lanes(j * 256, 256)
        for b in range(3):
            done = (acc_kv[b, :, to] + dot(nrm[b, :, half_two], w_in[half_two, cols], NN)).astype(bf16)
            for m in range(4):
                kv[m, pl.ds(b * 64, 64), to] = done[m * 64 : (m + 1) * 64]

    @pl.loop(0, 2)
    def _(j):
        cols = lanes(j * 256, 256)
        done = (acc_q[:, cols] + dot(nrm[1, :, half_two], w_in[half_two, cols], NN)).astype(bf16)
        q[:, cols] = (done.astype(f32) * 0.125).astype(bf16)

    go.x_two()
    masks = head_masks()
    att_send, att_recv = sems.run(8), sems.run(8)

    @pl.loop(0, 4)
    def _(m):
        rows = rows_at(m * 64, 64)
        for grp in range(2):
            cols = pl.ds(grp * 256, 256)
            q4 = spread_heads(q[rows, cols], masks)
            scores = dot(kv[m, :, cols], q4, NT)
            scores = jnp.where(mask[...] > 0.5, scores, masked_score)
            raised = jnp.exp(scores - jnp.max(scores, axis=0, keepdims=True))
            weights = raised * (1.0 / jnp.sum(raised, axis=0, keepdims=True))
            probs[m * 2 + grp] = weights
            mixed = dot(weights.astype(bf16), kv[m, :, pl.ds(512 + grp * 256, 256)], TN)
            to = lanes(grp * 512 + c * 256, 256)
            att[rows, to] = fold_heads(mixed, masks).astype(bf16)
            remote(att.at[rows, to], att.at[rows, to], att_send(m * 2 + grp), att_recv(m * 2 + grp), place.sibling())

    go.finish()

    def await_att(sem, col):
        @pl.loop(0, 4)
        def _(m):
            for grp in range(2):
                await_bytes(att.at[rows_at(m * 64, 64), lanes(grp * 512 + col * 256, 256)], sem(m * 2 + grp))

    await_att(att_recv, 1 - c)
    out_copies = []
    for j in range(2):
        cols = pl.ds(j * 256, 256)
        done = ens[1, :, lanes(c * 512 + j * 256, 256)].astype(f32) + dot(att[...], w_out[:, cols], NN)
        outs[0, :, cols] = done.astype(bf16)
        out_copies.append(
            remote(outs.at[0, :, cols], outs.at[1, :, cols], sems.take(), sems.take(), place.yoff(2))
        )

    @pl.loop(0, 8)
    def _(j):
        att_t[rows_at(j * 128, 128), :] = att[:, lanes(j * 128, 128)].T

    for copy in out_copies:
        copy.wait_recv()
    coef = (1.0 - (1.0 - fair_alpha) / 8) / 7

    @pl.loop(0, 8)
    def _(step):
        row = (step // 2) * 16
        cols = lanes((step % 2) * 256, 256)
        near = [outs[0, rows_at(m * 64 + row, 16), cols].astype(f32) for m in range(4)]
        far = [outs[1, rows_at(m * 64 + row, 16), cols].astype(f32) for m in range(4)]
        target = target_ref[rows_at(row, 16), lanes(c * 512 + (step % 2) * 256, 256)].astype(f32)
        spread = [None] * 4
        for m in range(4):
            for n in range(m + 1, 4):
                term = slope(near[m] - near[n])
                spread[m] = term if spread[m] is None else spread[m] + term
                spread[n] = -term if spread[n] is None else spread[n] - term
        for m in range(4):
            for n in range(4):
                spread[m] = spread[m] + slope(near[m] - far[n])
            cot[rows_at(m * 64 + row, 16), cols] = (slope(near[m] - target) - coef * spread[m]).astype(bf16)

    ga_copies = []
    for grp in range(2):
        cols = pl.ds(grp * 256, 256)
        ga_send[:, cols] = dot(cot[...], w_out[rows_at(grp * 512 + (1 - c) * 256, 256), :], NT)
        ga_copies.append(
            remote(ga_send.at[:, cols], ga_recv.at[:, cols], sems.take(), sems.take(), place.sibling())
        )
    to = lanes(c * 512, 512)
    cot_full[:, to] = cot[mine, :]
    cot_copy = remote(cot.at[theirs], cot_full.at[:, to], sems.take(), sems.take(), place.sibling())
    mine_ga = [dot(cot[...], w_out[rows_at(grp * 512 + c * 256, 256), :], NT) for grp in range(2)]
    for grp in range(2):
        cols = pl.ds(grp * 256, 256)
        ga_copies[grp].wait_recv()
        ga[:, cols] = (mine_ga[grp] + ga_recv[:, cols]).astype(bf16)

    def outer(part, left, right, first, count):
        width = 256

        @pl.loop(0, 2 * (count // width))
        def _(i):
            rows = rows_at(first + (i % 2) * 256, 256)
            cols = lanes((i // 2) * width, width)
            part[rows, cols] = dot(left[rows, :], right(cols), NN).astype(bf16)

    so = Scatter(place, part_o, y_o, x_o, l_o, z_o, sems)
    sq = Scatter(place, part_q, y_q, x_q, l_q, z_q, sems)
    sk = Scatter(place, part_k, y_k, x_k, l_k, z_k, sems)
    other_rows, mine_rows = (1 - yl) * 512, yl * 512
    cot_cols = lambda cols: cot[:, cols]
    outer(part_o, att_t, cot_cols, other_rows, 512)
    so.y_start()

    lo_send, lo_recv, hi_send, hi_recv = sems.run(4), sems.run(4), sems.run(4), sems.run(4)

    @pl.loop(0, 4)
    def _(m):
        rows = rows_at(m * 64, 64)
        for grp in range(2):
            cols = pl.ds(grp * 256, 256)
            vcols = pl.ds(512 + grp * 256, 256)
            q4 = spread_heads(q[rows, cols], masks)
            g4 = spread_heads(ga[rows, cols], masks)
            keys = kv[m, :, cols]
            weights = probs[m * 2 + grp]
            grad = dot(kv[m, :, vcols], g4, NT)
            inner = jnp.sum(weights * grad, axis=0, keepdims=True)
            grad_scores = (weights * (grad - inner)).astype(bf16)
            for at, value in (
                (vcols, dot(weights.astype(bf16), g4, NN)), (cols, dot(grad_scores, q4, NN))
            ):
                h_send[0, m, :, at] = value[0:64].astype(bf16)
                own_kv[rows, at] = value[64:128]
                h_send[1, m, :, at] = value[128:192].astype(bf16)
            gp[rows, cols] = (fold_heads(dot(grad_scores, keys, TN), masks) * 0.125).astype(bf16)
        remote(h_send.at[0, m], h_recv.at[0, m], lo_send(m), lo_recv(m), place.goff(-1))
        remote(h_send.at[1, m], h_recv.at[1, m], hi_send(m), hi_recv(m), place.goff(1))

    q_cols = lambda cols: gp[:, cols]
    outer(part_q, nrm_t, q_cols, other_rows, 512)
    sq.y_start()
    outer(part_o, att_t, cot_cols, mine_rows, 512)
    so.x_one()
    outer(part_q, nrm_t, q_cols, mine_rows, 512)
    so.x_two()

    @pl.loop(0, 4)
    def _(j):
        rows = rows_at(j * 256, 256)
        gn[:, lanes(j * 256, 256)] = dot(gp[:, pl.ds(0, 512)], w_in[rows, pl.ds(0, 512)], NT)

    sq.x_one()
    so.z_start()
    sq.x_two()

    @pl.loop(0, 4)
    def _(m):
        await_bytes(h_recv.at[0, m], lo_recv(m))
        await_bytes(h_recv.at[1, m], hi_recv(m))
        rows = rows_at(m * 64, 64)
        gp[rows, pl.ds(512, 1024)] = (
            own_kv[rows, :] + h_recv[0, m].astype(f32) + h_recv[1, m].astype(f32)
        ).astype(bf16)

    k_cols = lambda cols: gp[:, pl.ds(pl.multiple_of(512 + cols.start, 128), cols.size)]
    outer(part_k, nrm_t, k_cols, other_rows, 1024)
    sk.y_start()
    outer(part_k, nrm_t, k_cols, mine_rows, 1024)
    sq.z_start()
    pair_copies = []

    def settle(piece, start, count):
        at = pl.ds(start, count)
        pair[0, :, at] = piece.total().astype(bf16)
        pair_copies.append(
            remote(pair.at[0, :, at], pair.at[1, :, at], sems.take(), sems.take(), place.yoff(2))
        )

    settle(so, 1536, 512)

    @pl.loop(0, 4)
    def _(j):
        rows = rows_at(j * 256, 256)
        cols = lanes(j * 256, 256)
        gn[:, cols] = gn[:, cols] + dot(gp[:, pl.ds(512, 1024)], w_in[rows, pl.ds(512, 1024)], NT)

    gn_copy = remote(gn.at[theirs], gn_recv, sems.take(), sems.take(), place.sibling())
    settle(sq, 0, 512)
    sk.x_one()
    gn_copy.wait_recv()
    cot_copy.wait_recv()
    sk.x_two()

    @pl.loop(0, 8)
    def _(step):
        rows = rows_at(step * 16, 16)
        normed, inverse = normed_of(ens_ref[rows, :].astype(f32))
        summed = gn[rows_at(c * 128 + step * 16, 16), :] + gn_recv[rows, :]
        grad = jnp.concatenate([summed[:, spot(b) * 128 : (spot(b) + 1) * 128] for b in range(8)], axis=1)
        first = jnp.mean(grad, axis=-1, keepdims=True)
        second = jnp.mean(grad * normed, axis=-1, keepdims=True)
        gin_ref[rows, :] = (
            cot_full[rows, :].astype(f32) + inverse * (grad - first - normed * second)
        ).astype(bf16)

    sk.z_start()
    settle(sk, 512, 1024)
    for copy in pair_copies:
        copy.wait_recv()
    shared[0] = (pair[0].astype(f32) + pair[1].astype(f32)) * factor
    last = remote(shared.at[0], shared.at[1], sems.take(), sems.take(), place.sibling())

    def put(slot, side):
        for sec in range(3):
            for p in range(4):
                gwin_ref[:, lanes(sec * 1024 + side * 512 + PAIRS[p] * 128, 128)] = shared[
                    slot, :, pl.ds(sec * 512 + p * 128, 128)
                ]
        gwout_ref[:, lanes(side * 512, 512)] = shared[slot, :, pl.ds(1536, 512)]

    put(0, c)
    last.wait_recv()
    put(1, 1 - c)
    for copy in [ens_own, gn_copy, cot_copy, last] + out_copies + ga_copies + pair_copies:
        if copy is not ens_own:
            copy.wait_send()
    await_att(att_send, c)

    @pl.loop(0, 4)
    def _(m):
        await_bytes(h_send.at[0, m], lo_send(m))
        await_bytes(h_send.at[1, m], hi_send(m))

    for piece in (so, sq, sk):
        piece.finish()
    assert sems.used <= SEMS


def local(ensemble, target_field, weight_in, weight_out, window_start, window_end):
    mem_dev, points, width = ensemble.shape
    bf16, f32 = jnp.bfloat16, jnp.float32
    count = mem_dev * lax.axis_size("member") * points * lax.axis_size("grid")
    bounds = jnp.stack([jnp.tile(window_start, 4), jnp.tile(window_end, 4)])
    vmem = pl.BlockSpec(memory_space=pltpu.VMEM)

    def pieces(cols):
        return [
            pltpu.VMEM((1024, cols), bf16), pltpu.VMEM((512, cols), bf16), pltpu.VMEM((128, cols), bf16),
            pltpu.VMEM((2, 128, cols), bf16), pltpu.VMEM((8, 16, cols), bf16),
        ]

    grad_input, grad_in, grad_out = pl.pallas_call(
        functools.partial(whole_kernel, 1.0 / math.sqrt(count)),
        name="k_whole",
        out_shape=[
            jax.ShapeDtypeStruct((mem_dev * points, width), bf16),
            jax.ShapeDtypeStruct(weight_in.shape, f32),
            jax.ShapeDtypeStruct(weight_out.shape, f32),
        ],
        in_specs=[vmem] * 5,
        out_specs=[vmem] * 3,
        scratch_shapes=[
            pltpu.VMEM((1024, 1536), bf16),
            pltpu.VMEM((1024, 512), bf16),
            pltpu.VMEM((3, 256, 1024), bf16),
            pltpu.VMEM((3, 256, 1024), bf16),
            pltpu.VMEM((1024, 256), bf16),
            pltpu.VMEM((256, 512), bf16),
            pltpu.VMEM((4, 192, 1024), bf16),
            pltpu.VMEM((256, 512), f32),
            pltpu.VMEM((3, 256, 1024), f32),
            pltpu.VMEM((192, 256), f32),
            pltpu.VMEM((8, 192, 256), f32),
            pltpu.VMEM((256, 1024), bf16),
            pltpu.VMEM((1024, 256), bf16),
            pltpu.VMEM((2, 256, 512), bf16),
            pltpu.VMEM((256, 512), bf16),
            pltpu.VMEM((128, 1024), bf16),
            pltpu.VMEM((256, 512), f32),
            pltpu.VMEM((256, 512), f32),
            pltpu.VMEM((256, 512), bf16),
            pltpu.VMEM((256, 1536), bf16),
            pltpu.VMEM((256, 1024), f32),
            pltpu.VMEM((2, 4, 64, 1024), bf16),
            pltpu.VMEM((2, 4, 64, 1024), bf16),
            pltpu.VMEM((256, 1024), f32),
            pltpu.VMEM((128, 1024), f32),
        ]
        + pieces(512) + pieces(512) + pieces(1024)
        + [
            pltpu.VMEM((2, 16, 2048), bf16),
            pltpu.VMEM((2, 16, 2048), f32),
            pltpu.SemaphoreType.DMA((SEMS,)),
        ],
        compiler_params=pltpu.CompilerParams(
            collective_id=1, has_side_effects=True, vmem_limit_bytes=56 << 20
        ),
    )(ensemble.reshape(mem_dev * points, width), target_field, weight_in, weight_out, bounds)
    return grad_input.reshape(ensemble.shape), grad_in, grad_out


norm_eps = 1e-05
smooth_width = 0.1
fair_alpha = 0.95
masked_score = -1e30


def solution(mesh):
    in_specs = (
        P("member", "grid", None),
        P("grid", None),
        P("grid", None),
        P("grid", None),
        P("grid"),
        P("grid"),
    )
    out_specs = (P("member", "grid", None), P("grid", None), P("grid", None))
    return jax.shard_map(local, mesh=mesh, in_specs=in_specs, out_specs=out_specs, check_vma=False)
```

```python
import functools
import math

import jax
import jax.numpy as jnp
from jax import lax
from jax.experimental import pallas as pl
from jax.experimental.pallas import tpu as pltpu
from jax.sharding import PartitionSpec as P

MESH = pl.DeviceIdType.MESH


class Place:
    def __init__(self):
        g = lax.axis_index("grid")
        m = lax.axis_index("member")
        self.x, self.yl, self.z = g // 16, (g // 8) % 2, g % 8
        self.yh, self.c = m // 2, m % 2

    def dev(self, x, yl, z, yh, c):
        return (yh * 2 + c, (x * 2 + yl) * 8 + z)

    def zoff(self, s):
        return self.dev(self.x, self.yl, (self.z + s + 8) % 8, self.yh, self.c)

    def xoff(self, s):
        return self.dev((self.x + s + 4) % 4, self.yl, self.z, self.yh, self.c)

    def yoff(self, s):
        y = (2 * self.yh + self.yl + s + 4) % 4
        return self.dev(self.x, y % 2, self.z, y // 2, self.c)

    def sibling(self):
        return self.dev(self.x, self.yl, self.z, self.yh, 1 - self.c)

    def goff(self, s):
        g = ((self.x * 2 + self.yl) * 8 + self.z + s + 64) % 64
        return (self.yh * 2 + self.c, g)

    def far_sibling(self):
        return self.dev(self.x, self.yl, self.z, 1 - self.yh, 1 - self.c)

    def partners(self):
        return (
            [self.zoff(s) for s in range(1, 8)]
            + [self.xoff(s) for s in (1, -1, 2)]
            + [self.yoff(s) for s in (1, -1, 2)]
            + [self.sibling(), self.far_sibling(), self.goff(1), self.goff(-1)]
        )

    def signal(self):
        barrier = pltpu.get_barrier_semaphore()
        for partner in self.partners():
            pl.semaphore_signal(barrier, 1, device_id=partner, device_id_type=MESH)

    def await_all(self):
        pl.semaphore_wait(pltpu.get_barrier_semaphore(), len(self.partners()))


def remote(src, dst, send, recv, device):
    copy = pltpu.make_async_remote_copy(
        src_ref=src, dst_ref=dst, send_sem=send, recv_sem=recv, device_id=device, device_id_type=MESH
    )
    copy.start()
    return copy


def await_bytes(ref, sem):
    pltpu.make_async_copy(ref, ref, sem).wait()


def rows_at(start, count, unit=16):
    return pl.ds(pl.multiple_of(start, unit), count)


def lanes(start, count):
    return pl.ds(pl.multiple_of(start, 128), count)


def dot(a, b, dims):
    return lax.dot_general(a, b, (dims, ((), ())), preferred_element_type=jnp.float32)


NN = ((1,), (0,))
NT = ((1,), (1,))
TN = ((0,), (0,))


class Sems:
    def __init__(self, array):
        self.array, self.used = array, 0

    def take(self, count=None):
        start = self.used
        self.used += 1 if count is None else count
        if count is None:
            return self.array.at[start]
        return [self.array.at[start + i] for i in range(count)]

    def run(self, count):
        start = self.used
        self.used += count
        return lambda i: self.array.at[start + i]


def side_of(s):
    return 0 if s in (0, 1, 2, 3) else 1


class Gather:
    def __init__(self, place, buf, sems):
        self.place, self.buf, self.cols = place, buf, buf.shape[1]
        self.z_send, self.z_recv = sems.take(8), sems.take(8)
        self.x_send, self.x_recv, self.x_far = sems.take(2), [sems.take(8), sems.take(8)], sems.take(8)
        self.y_send, self.y_recv = sems.take(2), sems.take(2)
        self.z_copies = []

    def shard(self, xs, s):
        place = self.place
        start = place.yl * 512 + ((place.x + xs + 4) % 4) * 128 + ((place.z + s + 8) % 8) * 16
        return self.buf.at[rows_at(start, 16)]

    def to_y(self, ref, s):
        side = side_of(s)
        remote(ref, ref, self.y_send[side], self.y_recv[side], self.place.yoff(1 - 2 * side))

    def pass_on(self, s):
        ref, place = self.shard(0, s), self.place
        for way, sign in ((0, 1), (1, -1)):
            remote(ref, ref, self.x_send[way], self.x_recv[way][s % 8], place.xoff(sign))
        self.to_y(ref, s)

    def start(self):
        ref = self.shard(0, 0)
        for s in (1, -1, 2, -2, 3, -3, 4):
            self.z_copies.append(remote(ref, ref, self.z_send[s % 8], self.z_recv[-s % 8], self.place.zoff(s)))
        self.pass_on(0)

    def z_step(self, step):
        for s in sorted({-step, step} - {-4}):
            await_bytes(self.shard(0, s), self.z_recv[s % 8])
            self.pass_on(s)

    def x_step(self, step):
        for s in sorted({-step, step} - {-4}):
            for way, sign in ((0, 1), (1, -1)):
                ref = self.shard(-sign, s)
                await_bytes(ref, self.x_recv[way][s % 8])
                if side_of(s) == way:
                    remote(ref, ref, self.x_send[way], self.x_far[s % 8], self.place.xoff(sign))
                self.to_y(ref, s)

    def far_step(self, step):
        for s in sorted({-step, step} - {-4}):
            ref = self.shard(2, s)
            await_bytes(ref, self.x_far[s % 8])
            self.to_y(ref, s)

    def finish(self):
        for copy in self.z_copies:
            copy.wait_send()
        for side in range(2):
            await_bytes(self.buf.at[pl.ds(0, 256)], self.y_recv[side])
            await_bytes(self.buf.at[pl.ds(0, 192)], self.x_send[side])
            await_bytes(self.buf.at[pl.ds(0, 256)], self.y_send[side])


def add_rows(dst, src, start, count):
    dst[rows_at(start, count), :] = (
        dst[rows_at(start, count), :].astype(jnp.float32) + src.astype(jnp.float32)
    ).astype(dst.dtype)


class Scatter:
    def __init__(self, place, part, y_stage, x_stage, x_last, z_stage, sems):
        self.place, self.part, self.y_stage = place, part, y_stage
        self.x_stage, self.x_last, self.z_stage = x_stage, x_last, z_stage
        self.y_send, self.y_recv = sems.take(2), [sems.take(4), sems.take(4)]
        self.x_send, self.x_recv = sems.take(4), sems.take(4)
        self.z_send, self.z_recv = sems.take(8), sems.take(8)
        self.copies = []
        self.mine, self.other = place.yl * 512, (1 - place.yl) * 512

    def block(self, xs):
        return ((self.place.x + xs + 4) % 4) * 128

    def y_start(self):
        for index, xs in enumerate((2, 1, -1, 0)):
            for side, sign in ((0, 1), (1, -1)):
                start = self.block(xs) + side * 64
                remote(
                    self.part.at[rows_at(self.other + start, 64)], self.y_stage.at[rows_at(start, 64)],
                    self.y_send[side], self.y_recv[side][index], self.place.yoff(sign),
                )

    def take_y(self, index, xs):
        start = self.block(xs)
        for side in range(2):
            await_bytes(self.y_stage.at[rows_at(start + side * 64, 64)], self.y_recv[side][index])
        for sub in range(4):
            add_rows(self.part, self.y_stage[rows_at(start + sub * 32, 32), :], self.mine + start + sub * 32, 32)

    def x_one(self):
        self.take_y(0, 2)
        for way, sign in ((0, 1), (1, -1)):
            ref = self.part.at[rows_at(self.mine + self.block(2) + way * 64, 64)]
            self.copies.append(
                remote(ref, self.x_stage.at[pl.ds(way * 64, 64)], self.x_send[way], self.x_recv[way],
                       self.place.xoff(sign))
            )

    def x_two(self):
        for way, sign in ((0, 1), (1, -1)):
            self.take_y(1 + way, sign)
            self.copies[way].wait_recv()
            for sub in range(2):
                at = way * 64 + sub * 32
                add_rows(self.part, self.x_stage[pl.ds(at, 32), :], self.mine + self.block(sign) + at, 32)
            self.copies.append(
                remote(self.part.at[rows_at(self.mine + self.block(sign), 128)], self.x_last.at[way],
                       self.x_send[2 + way], self.x_recv[2 + way], self.place.xoff(sign))
            )

    def row(self, s):
        return rows_at(self.mine + self.block(0) + ((self.place.z + s) % 8) * 16, 16)

    def z_start(self):
        self.take_y(3, 0)
        for way in range(2):
            self.copies[2 + way].wait_recv()
        for sub in range(4):
            at = pl.ds(sub * 32, 32)
            both = self.x_last[0, at, :].astype(jnp.float32) + self.x_last[1, at, :].astype(jnp.float32)
            add_rows(self.part, both, self.mine + self.block(0) + sub * 32, 32)
        self.z_out()

    def z_out(self):
        self.z_copies = [
            remote(self.part.at[self.row(s)], self.z_stage.at[s], self.z_send[s], self.z_recv[s], self.place.zoff(s))
            for s in (4, 3, 5, 2, 6, 1, 7)
        ]

    def total(self):
        for copy in self.z_copies:
            copy.wait_recv()
        total = self.part[self.row(0), :].astype(jnp.float32)
        for s in range(1, 8):
            total = total + self.z_stage[s].astype(jnp.float32)
        return total

    def finish(self):
        for copy in self.copies + self.z_copies:
            copy.wait_send()
        for side in range(2):
            await_bytes(self.part.at[pl.ds(0, 256)], self.y_send[side])


SEMS = 306
class ScatterX(Scatter):
    def x_one(self):
        for way, sign in ((0, 1), (1, -1)):
            remote(self.part.at[rows_at(way * 512 + self.block(2), 128)], self.x_stage.at[pl.ds(way * 128, 128)],
                   self.x_send[way], self.x_recv[way], self.place.xoff(sign))

    def x_two(self):
        for way, sign in ((0, 1), (1, -1)):
            await_bytes(self.x_stage.at[pl.ds(way * 128, 128)], self.x_recv[way])
            add_rows(self.part, self.x_stage[pl.ds(way * 128, 128), :], way * 512 + self.block(sign), 128)
            for yl in range(2):
                remote(self.part.at[rows_at(yl * 512 + self.block(sign), 128)],
                       self.x_last.at[way, pl.ds(yl * 128, 128)],
                       self.x_send[2 + way], self.x_recv[2 + way], self.place.xoff(sign))

    def y_start(self):
        for way in range(2):
            await_bytes(self.x_last.at[way], self.x_recv[2 + way])
        for yl in range(2):
            at = pl.ds(yl * 128, 128)
            both = self.x_last[0, at, :].astype(jnp.float32) + self.x_last[1, at, :].astype(jnp.float32)
            add_rows(self.part, both, yl * 512 + self.block(0), 128)
        for side, sign in ((0, 1), (1, -1)):
            remote(self.part.at[rows_at(self.other + self.block(0) + side * 64, 64)],
                   self.y_stage.at[pl.ds(side * 64, 64)],
                   self.y_send[side], self.y_recv[side][0], self.place.yoff(sign))

    def z_start(self):
        for side in range(2):
            await_bytes(self.y_stage.at[pl.ds(side * 64, 64)], self.y_recv[side][0])
        add_rows(self.part, self.y_stage[...], self.mine + self.block(0), 128)
        self.z_out()

    def finish(self):
        for copy in self.z_copies:
            copy.wait_send()
        for way in range(2):
            await_bytes(self.part.at[pl.ds(0, 128)], self.x_send[way])
            await_bytes(self.part.at[pl.ds(0, 256)], self.x_send[2 + way])
            await_bytes(self.part.at[pl.ds(0, 64)], self.y_send[way])


GROUPS = ((0, 2), (1, 3))
LOCAL = [(0, p) for group in GROUPS for p in group] + [
    (sec, p) for group in GROUPS for sec in (1, 2) for p in group
]
PIECES = (
    [(3, p) for p in range(4)],
    [(sec, p) for sec in range(2) for p in GROUPS[0]],
    [(2, p) for p in GROUPS[0]],
    [(sec, p) for sec in range(2) for p in GROUPS[1]],
    [(2, p) for p in GROUPS[1]],
)
X_FIRST = (2, 4)


def spot(block):
    return (block % 2) * 4 + block // 2


def normed_of(wide):
    center = wide - jnp.mean(wide, axis=-1, keepdims=True)
    inverse = lax.rsqrt(jnp.mean(center * center, axis=-1, keepdims=True) + norm_eps)
    return center * inverse, inverse


def slope(delta):
    return delta * lax.rsqrt(delta * delta + smooth_width * smooth_width)


def head_masks():
    lane = lax.broadcasted_iota(jnp.int32, (64, 256), 1) // 64
    return [(lane == h).astype(jnp.float32) for h in range(4)]


def spread_heads(block, masks):
    wide = block.astype(jnp.float32)
    return jnp.concatenate([(wide * mask).astype(jnp.bfloat16) for mask in masks], axis=0)


def fold_heads(wide, masks):
    total = wide[0:64] * masks[0]
    for h in range(1, 4):
        total = total + wide[h * 64 : (h + 1) * 64] * masks[h]
    return total


def whole_kernel(
    factor, ens_ref, target_ref, win_ref, wout_ref, bounds_ref, gin_ref, gwin_ref, gwout_ref,
    w_all, ens, nrm, nrm_t, q, kv, acc_q, acc_kv, mask, probs, att, att_t, outs, cot, cot_full,
    ga_send, ga_recv, ga, gq, own_kv, gkv, h_recv, gn, gn_recv, *rest,
):
    *stages, pair, sem_array = rest
    place = Place()
    sems = Sems(sem_array)
    c, yl = place.c, place.yl
    own = yl * 512 + place.x * 128 + place.z * 16
    bf16, f32 = jnp.bfloat16, jnp.float32
    place.signal()
    for t, (sec, p) in enumerate(LOCAL):
        w_all[rows_at(own, 16), pl.ds(t * 128, 128)] = win_ref[:, lanes(sec * 1024 + c * 512 + p * 128, 128)]
    w_all[rows_at(own, 16), pl.ds(1536, 512)] = wout_ref[:, lanes(c * 512, 512)]
    ens[1, rows_at(c * 128, 128), :] = ens_ref[...]

    def norm_rows(b, core):
        @pl.loop(0, 4)
        def _(step):
            rows = rows_at(core * 128 + step * 32, 32)
            normed = normed_of(ens[b, rows, :].astype(f32))[0].astype(bf16)
            for block in range(8):
                nrm[b, rows, pl.ds(spot(block) * 128, 128)] = normed[:, block * 128 : (block + 1) * 128]

    norm_rows(1, c)
    place.await_all()
    gi = Gather(place, w_all, sems)
    gi.start()
    mine = rows_at(c * 128, 128)
    theirs = rows_at((1 - c) * 128, 128)
    ens_own = remote(ens_ref, ens.at[1, mine], sems.take(), sems.take(), place.sibling())
    position = place.goff(0)[1] * 64 - 64 + lax.broadcasted_iota(jnp.int32, (192, 256), 0)
    valid = (position >= bounds_ref[0:1, :]) & (position < bounds_ref[1:2, :])
    mask[...] = valid.astype(f32)
    gi.z_step(1)
    gi.x_step(0)
    gi.z_step(2)
    gi.x_step(1)
    gi.far_step(0)
    gi.z_step(3)
    halo = [
        remote(ens_ref, ens.at[0, mine], sems.take(), sems.take(), place.goff(1)),
        remote(ens_ref, ens.at[2, mine], sems.take(), sems.take(), place.goff(-1)),
    ]
    gi.x_step(2)
    gi.far_step(1)
    ens_own.wait()
    norm_rows(1, 1 - c)
    gi.z_step(4)
    gi.x_step(3)
    gi.far_step(2)

    gi.x_step(4)
    gi.far_step(3)
    gi.far_step(4)
    half_one, half_two = lanes(yl * 512, 512), lanes((1 - yl) * 512, 512)

    def first_half(b):
        @pl.loop(0, 4)
        def _(j):
            acc_kv[b, :, lanes(j * 256, 256)] = dot(nrm[b, :, half_one], w_all[half_one, lanes(512 + j * 256, 256)], NN)

    first_half(1)

    @pl.loop(0, 2)
    def _(j):
        cols = lanes(j * 256, 256)
        acc_q[:, cols] = dot(nrm[1, :, half_one], w_all[half_one, cols], NN)

    for copy in halo:
        copy.wait_recv()
    onward = [
        remote(ens.at[b, mine], ens.at[b, mine], sems.take(), sems.take(), place.sibling()) for b in (0, 2)
    ]
    norm_rows(0, c)
    norm_rows(2, c)
    for copy in onward:
        copy.wait()
    for copy in halo:
        copy.wait_send()
    norm_rows(0, 1 - c)
    norm_rows(2, 1 - c)

    @pl.loop(0, 2)
    def _(t):
        first_half(2 * t)

    gi.finish()

    @pl.loop(0, 4)
    def _(j):
        cols = lanes(512 + j * 256, 256)
        to = lanes(j * 256, 256)
        for b in range(3):
            done = (acc_kv[b, :, to] + dot(nrm[b, :, half_two], w_all[half_two, cols], NN)).astype(bf16)
            for m in range(4):
                kv[m, pl.ds(b * 64, 64), to] = done[m * 64 : (m + 1) * 64]

    @pl.loop(0, 2)
    def _(j):
        cols = lanes(j * 256, 256)
        done = (acc_q[:, cols] + dot(nrm[1, :, half_two], w_all[half_two, cols], NN)).astype(bf16)
        q[:, cols] = (done.astype(f32) * 0.125).astype(bf16)

    masks = head_masks()
    att_send, att_recv = sems.run(8), sems.run(8)

    @pl.loop(0, 4)
    def _(m):
        rows = rows_at(m * 64, 64)
        for grp in range(2):
            cols = pl.ds(grp * 256, 256)
            q4 = spread_heads(q[rows, cols], masks)
            scores = dot(kv[m, :, pl.ds(grp * 512, 256)], q4, NT)
            scores = jnp.where(mask[...] > 0.5, scores, masked_score)
            raised = jnp.exp(scores - jnp.max(scores, axis=0, keepdims=True))
            weights = raised * (1.0 / jnp.sum(raised, axis=0, keepdims=True))
            probs[m * 2 + grp] = weights
            mixed = dot(weights.astype(bf16), kv[m, :, pl.ds(grp * 512 + 256, 256)], TN)
            to = lanes(grp * 512 + c * 256, 256)
            att[rows, to] = fold_heads(mixed, masks).astype(bf16)
            remote(att.at[rows, to], att.at[rows, to], att_send(m * 2 + grp), att_recv(m * 2 + grp), place.sibling())


    def await_att(sem, col):
        @pl.loop(0, 4)
        def _(m):
            for grp in range(2):
                await_bytes(att.at[rows_at(m * 64, 64), lanes(grp * 512 + col * 256, 256)], sem(m * 2 + grp))

    await_att(att_recv, 1 - c)
    out_copies = []
    for j in range(2):
        cols = pl.ds(j * 256, 256)
        done = ens[1, :, lanes(c * 512 + j * 256, 256)].astype(f32) + dot(att[...], w_all[:, pl.ds(1536 + j * 256, 256)], NN)
        outs[0, :, cols] = done.astype(bf16)
        out_copies.append(
            remote(outs.at[0, :, cols], outs.at[1, :, cols], sems.take(), sems.take(), place.yoff(2))
        )

    @pl.loop(0, 8)
    def _(j):
        rows = rows_at(j * 128, 128)
        cols = lanes(j * 128, 128)
        att_t[rows, :] = att[:, cols].T
        for b in range(3):
            nrm_t[rows, pl.ds(b * 256, 256)] = nrm[b, :, cols].T

    coef = (1.0 - (1.0 - fair_alpha) / 8) / 7
    for j in range(2):
        cols = pl.ds(j * 256, 256)
        out_copies[j].wait_recv()

        @pl.loop(0, 4)
        def _(step):
            row = step * 16
            near = [outs[0, rows_at(m * 64 + row, 16), cols].astype(f32) for m in range(4)]
            far = [outs[1, rows_at(m * 64 + row, 16), cols].astype(f32) for m in range(4)]
            target = target_ref[rows_at(row, 16), lanes(c * 512 + j * 256, 256)].astype(f32)
            spread = [None] * 4
            for m in range(4):
                for n in range(m + 1, 4):
                    term = slope(near[m] - near[n])
                    spread[m] = term if spread[m] is None else spread[m] + term
                    spread[n] = -term if spread[n] is None else spread[n] - term
            for m in range(4):
                for n in range(4):
                    spread[m] = spread[m] + slope(near[m] - far[n])
                cot[rows_at(m * 64 + row, 16), cols] = (slope(near[m] - target) - coef * spread[m]).astype(bf16)


    def back_out(start):
        rows = rows_at(start, 256)
        return dot(cot[...], w_all[rows, pl.ds(1536, 512)], NT)

    ga_copies = []
    for grp in range(2):
        cols = pl.ds(grp * 256, 256)
        ga_send[:, cols] = back_out(grp * 512 + (1 - c) * 256)
        ga_copies.append(
            remote(ga_send.at[:, cols], ga_recv.at[:, cols], sems.take(), sems.take(), place.sibling())
        )
    to = lanes(c * 512, 512)
    cot_full[:, to] = cot[mine, :]
    cot_copy = remote(cot.at[theirs], cot_full.at[:, to], sems.take(), sems.take(), place.sibling())
    mine_ga = [back_out(grp * 512 + c * 256) for grp in range(2)]
    for grp in range(2):
        cols = pl.ds(grp * 256, 256)
        ga_copies[grp].wait_recv()
        ga[:, cols] = (mine_ga[grp] + ga_recv[:, cols]).astype(bf16)

    pieces = [
        (ScatterX if i in X_FIRST else Scatter)(place, *stages[i * 5 : i * 5 + 5], sems) for i in range(len(PIECES))
    ]
    so, s0, v0, sa, v1 = pieces
    other_rows, mine_rows = (1 - yl) * 512, yl * 512
    mid = pl.ds(256, 256)

    def outer(piece, first, terms, parts=2):
        @pl.loop(0, parts)
        def _(i):
            rows = rows_at(first + i * 256, 256)
            for t, (left, inner, right, start) in enumerate(terms):
                piece.part[rows, pl.ds(t * 256, 256)] = dot(
                    left[rows, inner], right[:, pl.ds(start, 256)], NN
                ).astype(bf16)

    every = pl.ds(0, 768)
    all_o = [(att_t, pl.ds(0, 256), cot, 0), (att_t, pl.ds(0, 256), cot, 256)]
    all_q = [(nrm_t, mid, gq, 0), (nrm_t, mid, gq, 256)]
    all_kv = [(nrm_t, every, gkv, t * 256) for t in range(4)]
    all_0 = [all_q[0], all_kv[0]]
    all_a = [all_q[1], all_kv[2]]
    outer(so, other_rows, all_o)
    so.y_start()
    halos = []

    def back(grp):
        cols = pl.ds(grp * 256, 256)
        kcols = pl.ds(grp * 512, 256)
        vcols = pl.ds(grp * 512 + 256, 256)

        @pl.loop(0, 4)
        def _(m):
            rows = rows_at(m * 64, 64)
            q4 = spread_heads(q[rows, cols], masks)
            g4 = spread_heads(ga[rows, cols], masks)
            keys = kv[m, :, kcols]
            weights = probs[m * 2 + grp]
            grad = dot(kv[m, :, vcols], g4, NT)
            inner = jnp.sum(weights * grad, axis=0, keepdims=True)
            grad_scores = (weights * (grad - inner)).astype(bf16)
            for at, value in (
                (vcols, dot(weights.astype(bf16), g4, NN)), (kcols, dot(grad_scores, q4, NN))
            ):
                own_kv[rows, at] = value[64:128]
                rounded = value.astype(bf16)
                for b in range(3):
                    gkv[rows_at(b * 256 + m * 64, 64), at] = rounded[b * 64 : (b + 1) * 64]
            gq[rows, cols] = (fold_heads(dot(grad_scores, keys, TN), masks) * 0.125).astype(bf16)

    def send_halo(grp):
        at = pl.ds(grp * 512, 512)
        halos.append(
            [
                remote(gkv.at[pl.ds(0, 256), at], h_recv.at[0, :, at], sems.take(), sems.take(), place.goff(-1)),
                remote(gkv.at[pl.ds(512, 256), at], h_recv.at[1, :, at], sems.take(), sems.take(), place.goff(1)),
            ]
        )

    back(0)
    outer(s0, other_rows, all_0)
    s0.y_start()
    send_halo(0)
    outer(v0, 0, [all_kv[1]], 4)
    v0.x_one()
    outer(so, mine_rows, all_o)
    so.x_one()
    back(1)
    outer(sa, other_rows, all_a)
    sa.y_start()
    outer(v1, 0, [all_kv[3]], 4)
    v1.x_one()
    send_halo(1)
    so.x_two()
    v0.x_two()
    outer(s0, mine_rows, all_0)
    s0.x_one()
    outer(sa, mine_rows, all_a)
    @pl.loop(0, 4)
    def _(j):
        rows = rows_at(j * 256, 256)
        gn[:, lanes(j * 256, 256)] = dot(gq[...], w_all[rows, pl.ds(0, 512)], NT)

    v1.x_two()
    so.z_start()
    v0.y_start()
    s0.x_two()
    pair_copies = {}
    starts = [0]
    for blocks in PIECES:
        starts.append(starts[-1] + len(blocks) * 128)

    def settle(i):
        at = pl.ds(starts[i], starts[i + 1] - starts[i])
        pair[0, :, at] = pieces[i].total().astype(bf16)
        pair_copies[i] = [
            remote(pair.at[0, :, at], pair.at[slot, :, at], sems.take(), sems.take(), device)
            for slot, device in ((3, place.far_sibling()), (1, place.yoff(2)), (2, place.sibling()))
        ]

    def deliver(i):
        for copy in pair_copies[i]:
            copy.wait_recv()
        for side, slot in ((c, 0), (1 - c, 2)):
            for t, (sec, p) in enumerate(PIECES[i]):
                at = pl.ds(starts[i] + t * 128, 128)
                value = (pair[slot, :, at].astype(f32) + pair[slot + 1, :, at].astype(f32)) * factor
                if sec == 3:
                    gwout_ref[:, lanes(side * 512 + p * 128, 128)] = value
                else:
                    gwin_ref[:, lanes(sec * 1024 + side * 512 + p * 128, 128)] = value

    sa.x_one()
    v1.y_start()
    v0.z_start()
    s0.z_start()
    settle(0)
    sa.x_two()
    v1.z_start()
    for pair_halo in halos:
        for copy in pair_halo:
            copy.wait()
    for grp in range(2):
        @pl.loop(0, 4)
        def _(m):
            rows = rows_at(m * 64, 64)
            at = pl.ds(grp * 512, 512)
            gkv[rows_at(256 + m * 64, 64), at] = (
                own_kv[rows, at] + h_recv[0, rows, at].astype(f32) + h_recv[1, rows, at].astype(f32)
            ).astype(bf16)

    @pl.loop(0, 4)
    def _(j):
        rows = rows_at(j * 256, 256)
        cols = lanes(j * 256, 256)
        gn[:, cols] = gn[:, cols] + dot(gkv[pl.ds(256, 256), :], w_all[rows, pl.ds(512, 1024)], NT)

    gn_copy = remote(gn.at[theirs], gn_recv, sems.take(), sems.take(), place.sibling())
    sa.z_start()
    settle(2)
    settle(1)
    settle(4)
    deliver(0)
    gn_copy.wait_recv()
    cot_copy.wait_recv()

    @pl.loop(0, 8)
    def _(step):
        rows = rows_at(step * 16, 16)
        normed, inverse = normed_of(ens_ref[rows, :].astype(f32))
        summed = gn[rows_at(c * 128 + step * 16, 16), :] + gn_recv[rows, :]
        grad = jnp.concatenate([summed[:, spot(b) * 128 : (spot(b) + 1) * 128] for b in range(8)], axis=1)
        first = jnp.mean(grad, axis=-1, keepdims=True)
        second = jnp.mean(grad * normed, axis=-1, keepdims=True)
        gin_ref[rows, :] = (
            cot_full[rows, :].astype(f32) + inverse * (grad - first - normed * second)
        ).astype(bf16)

    settle(3)
    for i in (2, 1, 4, 3):
        deliver(i)
    for copy in [gn_copy, cot_copy] + out_copies + ga_copies + sum(pair_copies.values(), []):
        copy.wait_send()
    await_att(att_send, c)
    for piece in pieces:
        piece.finish()
    assert sems.used <= SEMS


def local(ensemble, target_field, weight_in, weight_out, window_start, window_end):
    mem_dev, points, width = ensemble.shape
    bf16, f32 = jnp.bfloat16, jnp.float32
    count = mem_dev * lax.axis_size("member") * points * lax.axis_size("grid")
    bounds = jnp.stack([jnp.tile(window_start, 4), jnp.tile(window_end, 4)])
    vmem = pl.BlockSpec(memory_space=pltpu.VMEM)
    stages = [
        pltpu.VMEM(shape + (len(blocks) * 128,), bf16)
        for i, blocks in enumerate(PIECES)
        for shape in (
            ((1024,), (128,), (256,), (2, 256), (8, 16)) if i in X_FIRST else ((1024,), (512,), (128,), (2, 128), (8, 16))
        )
    ]

    grad_input, grad_in, grad_out = pl.pallas_call(
        functools.partial(whole_kernel, 1.0 / math.sqrt(count)),
        name="k_whole",
        out_shape=[
            jax.ShapeDtypeStruct((mem_dev * points, width), bf16),
            jax.ShapeDtypeStruct(weight_in.shape, f32),
            jax.ShapeDtypeStruct(weight_out.shape, f32),
        ],
        in_specs=[vmem] * 5,
        out_specs=[vmem] * 3,
        scratch_shapes=[
            pltpu.VMEM((1024, 2048), bf16),
            pltpu.VMEM((3, 256, 1024), bf16),
            pltpu.VMEM((3, 256, 1024), bf16),
            pltpu.VMEM((1024, 768), bf16),
            pltpu.VMEM((256, 512), bf16),
            pltpu.VMEM((4, 192, 1024), bf16),
            pltpu.VMEM((256, 512), f32),
            pltpu.VMEM((3, 256, 1024), f32),
            pltpu.VMEM((192, 256), f32),
            pltpu.VMEM((8, 192, 256), f32),
            pltpu.VMEM((256, 1024), bf16),
            pltpu.VMEM((1024, 256), bf16),
            pltpu.VMEM((2, 256, 512), bf16),
            pltpu.VMEM((256, 512), bf16),
            pltpu.VMEM((128, 1024), bf16),
            pltpu.VMEM((256, 512), f32),
            pltpu.VMEM((256, 512), f32),
            pltpu.VMEM((256, 512), bf16),
            pltpu.VMEM((256, 512), bf16),
            pltpu.VMEM((256, 1024), f32),
            pltpu.VMEM((768, 1024), bf16),
            pltpu.VMEM((2, 256, 1024), bf16),
            pltpu.VMEM((256, 1024), f32),
            pltpu.VMEM((128, 1024), f32),
        ]
        + stages
        + [
            pltpu.VMEM((4, 16, 2048), bf16),
            pltpu.SemaphoreType.DMA((SEMS,)),
        ],
        compiler_params=pltpu.CompilerParams(
            collective_id=1, has_side_effects=True, vmem_limit_bytes=56 << 20
        ),
    )(ensemble.reshape(mem_dev * points, width), target_field, weight_in, weight_out, bounds)
    return grad_input.reshape(ensemble.shape), grad_in, grad_out


norm_eps = 1e-05
smooth_width = 0.1
fair_alpha = 0.95
masked_score = -1e30


def solution(mesh):
    in_specs = (
        P("member", "grid", None),
        P("grid", None),
        P("grid", None),
        P("grid", None),
        P("grid"),
        P("grid"),
    )
    out_specs = (P("member", "grid", None), P("grid", None), P("grid", None))
    return jax.shard_map(local, mesh=mesh, in_specs=in_specs, out_specs=out_specs, check_vma=False)
```

```python
import functools
import math

import jax
import jax.numpy as jnp
from jax import lax
from jax.experimental import pallas as pl
from jax.experimental.pallas import tpu as pltpu
from jax.sharding import PartitionSpec as P

MESH = pl.DeviceIdType.MESH


class Place:
    def __init__(self):
        g = lax.axis_index("grid")
        m = lax.axis_index("member")
        self.x, self.yl, self.z = g // 16, (g // 8) % 2, g % 8
        self.yh, self.c = m // 2, m % 2

    def dev(self, x, yl, z, yh, c):
        return (yh * 2 + c, (x * 2 + yl) * 8 + z)

    def zoff(self, s):
        return self.dev(self.x, self.yl, (self.z + s + 8) % 8, self.yh, self.c)

    def xoff(self, s):
        return self.dev((self.x + s + 4) % 4, self.yl, self.z, self.yh, self.c)

    def yoff(self, s):
        y = (2 * self.yh + self.yl + s + 4) % 4
        return self.dev(self.x, y % 2, self.z, y // 2, self.c)

    def sibling(self):
        return self.dev(self.x, self.yl, self.z, self.yh, 1 - self.c)

    def goff(self, s):
        g = ((self.x * 2 + self.yl) * 8 + self.z + s + 64) % 64
        return (self.yh * 2 + self.c, g)

    def far_sibling(self):
        return self.dev(self.x, self.yl, self.z, 1 - self.yh, 1 - self.c)

    def partners(self):
        return (
            [self.zoff(s) for s in range(1, 8)]
            + [self.xoff(s) for s in (1, -1, 2)]
            + [self.yoff(s) for s in (1, -1, 2)]
            + [self.sibling(), self.far_sibling(), self.goff(1), self.goff(-1)]
        )

    def signal(self):
        barrier = pltpu.get_barrier_semaphore()
        for partner in self.partners():
            pl.semaphore_signal(barrier, 1, device_id=partner, device_id_type=MESH)

    def await_all(self):
        pl.semaphore_wait(pltpu.get_barrier_semaphore(), len(self.partners()))


def remote(src, dst, send, recv, device):
    copy = pltpu.make_async_remote_copy(
        src_ref=src, dst_ref=dst, send_sem=send, recv_sem=recv, device_id=device, device_id_type=MESH
    )
    copy.start()
    return copy


def await_bytes(ref, sem):
    pltpu.make_async_copy(ref, ref, sem).wait()


def rows_at(start, count, unit=16):
    return pl.ds(pl.multiple_of(start, unit), count)


def lanes(start, count):
    return pl.ds(pl.multiple_of(start, 128), count)


def dot(a, b, dims):
    return lax.dot_general(a, b, (dims, ((), ())), preferred_element_type=jnp.float32)


NN = ((1,), (0,))
NT = ((1,), (1,))
TN = ((0,), (0,))


class Sems:
    def __init__(self, array):
        self.array, self.used = array, 0

    def take(self, count=None):
        start = self.used
        self.used += 1 if count is None else count
        if count is None:
            return self.array.at[start]
        return [self.array.at[start + i] for i in range(count)]

    def run(self, count):
        start = self.used
        self.used += count
        return lambda i: self.array.at[start + i]


def side_of(s):
    return 0 if s in (0, 1, 2, 3) else 1


class Gather:
    def __init__(self, place, buf, sems):
        self.place, self.buf, self.cols = place, buf, buf.shape[1]
        self.z_send, self.z_recv = sems.take(8), sems.take(8)
        self.x_send, self.x_recv, self.x_far = sems.take(2), [sems.take(8), sems.take(8)], sems.take(8)
        self.y_send, self.y_recv = sems.take(2), sems.take(2)
        self.z_copies = []

    def shard(self, xs, s):
        place = self.place
        start = place.yl * 512 + ((place.x + xs + 4) % 4) * 128 + ((place.z + s + 8) % 8) * 16
        return self.buf.at[rows_at(start, 16)]

    def to_y(self, ref, s):
        side = side_of(s)
        remote(ref, ref, self.y_send[side], self.y_recv[side], self.place.yoff(1 - 2 * side))

    def pass_on(self, s):
        ref, place = self.shard(0, s), self.place
        for way, sign in ((0, 1), (1, -1)):
            remote(ref, ref, self.x_send[way], self.x_recv[way][s % 8], place.xoff(sign))
        self.to_y(ref, s)

    def start(self):
        ref = self.shard(0, 0)
        for s in (1, -1, 2, -2, 3, -3, 4):
            self.z_copies.append(remote(ref, ref, self.z_send[s % 8], self.z_recv[-s % 8], self.place.zoff(s)))
        self.pass_on(0)

    def z_step(self, step):
        for s in sorted({-step, step} - {-4}):
            await_bytes(self.shard(0, s), self.z_recv[s % 8])
            self.pass_on(s)

    def x_step(self, step):
        for s in sorted({-step, step} - {-4}):
            for way, sign in ((0, 1), (1, -1)):
                ref = self.shard(-sign, s)
                await_bytes(ref, self.x_recv[way][s % 8])
                if side_of(s) == way:
                    remote(ref, ref, self.x_send[way], self.x_far[s % 8], self.place.xoff(sign))
                self.to_y(ref, s)

    def far_step(self, step):
        for s in sorted({-step, step} - {-4}):
            ref = self.shard(2, s)
            await_bytes(ref, self.x_far[s % 8])
            self.to_y(ref, s)

    def finish(self):
        for copy in self.z_copies:
            copy.wait_send()
        for side in range(2):
            await_bytes(self.buf.at[pl.ds(0, 256)], self.y_recv[side])
            await_bytes(self.buf.at[pl.ds(0, 192)], self.x_send[side])
            await_bytes(self.buf.at[pl.ds(0, 256)], self.y_send[side])


def add_rows(dst, start, count, *sources):
    @pl.loop(0, count // 32)
    def _(step):
        rows = rows_at(start + step * 32, 32)
        total = dst[rows, :].astype(jnp.float32)
        for ref, first in sources:
            total = total + ref[rows_at(first + step * 32, 32), :].astype(jnp.float32)
        dst[rows, :] = total.astype(dst.dtype)


class Scatter:
    def __init__(self, place, part, y_stage, x_stage, x_last, z_stage, sems):
        self.place, self.part, self.y_stage = place, part, y_stage
        self.x_stage, self.x_last, self.z_stage = x_stage, x_last, z_stage
        self.y_send, self.y_recv = sems.take(2), [sems.run(4), sems.run(4)]
        self.x_send, self.x_recv = sems.take(4), sems.take(4)
        self.z_send, self.z_recv = sems.run(8), sems.run(8)
        self.mine, self.other = place.yl * 512, (1 - place.yl) * 512

    def block(self, xs):
        return ((self.place.x + xs + 4) % 4) * 128

    def y_start(self):
        @pl.loop(0, 4)
        def _(index):
            start = self.block(jnp.where(index == 2, 3, jnp.where(index == 3, 0, 2 - index)))
            for side, sign in ((0, 1), (1, -1)):
                at = start + side * 64
                remote(
                    self.part.at[rows_at(self.other + at, 64)], self.y_stage.at[rows_at(at, 64)],
                    self.y_send[side], self.y_recv[side](index), self.place.yoff(sign),
                )

    def take_y(self, index, xs):
        start = self.block(xs)
        for side in range(2):
            await_bytes(self.y_stage.at[rows_at(start + side * 64, 64)], self.y_recv[side](index))
        add_rows(self.part, self.mine + start, 128, (self.y_stage, start))

    def x_one(self):
        for index, xs in enumerate((2, 1, -1)):
            self.take_y(index, xs)
            remote(self.part.at[rows_at(self.mine + self.block(xs), 128)], self.x_last.at[index],
                   self.x_send[index], self.x_recv[index], self.place.xoff(xs))

    def row(self, s):
        return rows_at(self.mine + self.block(0) + ((self.place.z + s) % 8) * 16, 16)

    def z_start(self):
        self.take_y(3, 0)
        for index in range(3):
            await_bytes(self.x_last.at[index], self.x_recv[index])
        add_rows(self.part, self.mine + self.block(0), 128, *[(self.x_last.at[index], 0) for index in range(3)])
        self.z_out()

    def z_out(self):
        @pl.loop(1, 8)
        def _(s):
            remote(self.part.at[self.row(s)], self.z_stage.at[s], self.z_send(s), self.z_recv(s), self.place.zoff(s))

    def z_drain(self):
        @pl.loop(1, 8)
        def _(s):
            await_bytes(self.part.at[pl.ds(0, 16)], self.z_send(s))

    def total(self):
        @pl.loop(1, 8)
        def _(s):
            await_bytes(self.z_stage.at[s], self.z_recv(s))

        total = self.part[self.row(0), :].astype(jnp.float32)
        for s in range(1, 8):
            total = total + self.z_stage[s].astype(jnp.float32)
        return total

    def finish(self):
        self.z_drain()
        for index in range(3):
            await_bytes(self.part.at[pl.ds(0, 128)], self.x_send[index])
        for side in range(2):
            await_bytes(self.part.at[pl.ds(0, 256)], self.y_send[side])


SEMS = 312
class ScatterX(Scatter):
    def x_one(self):
        for way, sign in ((0, 1), (1, -1)):
            remote(self.part.at[rows_at(way * 512 + self.block(2), 128)], self.x_stage.at[pl.ds(way * 128, 128)],
                   self.x_send[way], self.x_recv[way], self.place.xoff(sign))

    def x_two(self):
        for way, sign in ((0, 1), (1, -1)):
            await_bytes(self.x_stage.at[pl.ds(way * 128, 128)], self.x_recv[way])
            add_rows(self.part, way * 512 + self.block(sign), 128, (self.x_stage, way * 128))
            for yl in range(2):
                remote(self.part.at[rows_at(yl * 512 + self.block(sign), 128)],
                       self.x_last.at[way, pl.ds(yl * 128, 128)],
                       self.x_send[2 + way], self.x_recv[2 + way], self.place.xoff(sign))

    def y_start(self):
        for way in range(2):
            await_bytes(self.x_last.at[way], self.x_recv[2 + way])
        for yl in range(2):
            last = [(self.x_last.at[way], yl * 128) for way in range(2)]
            add_rows(self.part, yl * 512 + self.block(0), 128, *last)
        for side, sign in ((0, 1), (1, -1)):
            remote(self.part.at[rows_at(self.other + self.block(0) + side * 64, 64)],
                   self.y_stage.at[pl.ds(side * 64, 64)],
                   self.y_send[side], self.y_recv[side](0), self.place.yoff(sign))

    def z_start(self):
        for side in range(2):
            await_bytes(self.y_stage.at[pl.ds(side * 64, 64)], self.y_recv[side](0))
        add_rows(self.part, self.mine + self.block(0), 128, (self.y_stage, 0))
        self.z_out()

    def finish(self):
        self.z_drain()
        for way in range(2):
            await_bytes(self.part.at[pl.ds(0, 128)], self.x_send[way])
            await_bytes(self.part.at[pl.ds(0, 256)], self.x_send[2 + way])
            await_bytes(self.part.at[pl.ds(0, 64)], self.y_send[way])


GROUPS = ((0, 2), (1, 3))
LOCAL = [(0, p) for group in GROUPS for p in group] + [
    (sec, p) for group in GROUPS for sec in (1, 2) for p in group
]
PIECES = (
    [(3, p) for p in range(4)],
    [(sec, p) for sec in range(2) for p in GROUPS[0]],
    [(2, p) for p in GROUPS[0]],
    [(sec, p) for sec in range(2) for p in GROUPS[1]],
    [(2, p) for p in GROUPS[1]],
)
X_FIRST = (2, 4)


def spot(block):
    return (block % 2) * 4 + block // 2


def normed_of(wide):
    center = wide - jnp.mean(wide, axis=-1, keepdims=True)
    inverse = lax.rsqrt(jnp.mean(center * center, axis=-1, keepdims=True) + norm_eps)
    return center * inverse, inverse


def slope(delta):
    return delta * lax.rsqrt(delta * delta + smooth_width * smooth_width)


def head_masks():
    lane = lax.broadcasted_iota(jnp.int32, (64, 256), 1) // 64
    return [(lane == h).astype(jnp.float32) for h in range(4)]


def spread_heads(block, masks):
    wide = block.astype(jnp.float32)
    return jnp.concatenate([(wide * mask).astype(jnp.bfloat16) for mask in masks], axis=0)


def fold_heads(wide, masks):
    total = wide[0:64] * masks[0]
    for h in range(1, 4):
        total = total + wide[h * 64 : (h + 1) * 64] * masks[h]
    return total


def whole_kernel(
    factor, ens_hbm, target_hbm, win_hbm, wout_hbm, start_ref, end_ref, gin_ref, gwin_ref, gwout_ref,
    target_ref, win_ref, wout_ref,
    w_all, ens, nrm, nrm_t, q, kv, acc_q, acc_kv, mask, probs, att, att_t, outs, cot, cot_full,
    ga_part, ga_recv, ga, gq, own_kv, gkv, h_recv, gn, gn_recv, *rest,
):
    *stages, pair, sem_array = rest
    place = Place()
    sems = Sems(sem_array)
    c, yl = place.c, place.yl
    own = yl * 512 + place.x * 128 + place.z * 16
    bf16, f32 = jnp.bfloat16, jnp.float32
    place.signal()
    mine = rows_at(c * 128, 128)
    theirs = rows_at((1 - c) * 128, 128)
    loads = [
        pltpu.make_async_copy(src, dst, sems.take())
        for src, dst in (
            (win_hbm, win_ref), (wout_hbm, wout_ref), (ens_hbm, ens.at[1, mine]), (target_hbm, target_ref)
        )
    ]
    for load in loads:
        load.start()
    for load in loads[:2]:
        load.wait()
    for t, (sec, p) in enumerate(LOCAL):
        w_all[rows_at(own, 16), pl.ds(t * 128, 128)] = win_ref[:, lanes(sec * 1024 + c * 512 + p * 128, 128)]
    w_all[rows_at(own, 16), pl.ds(1536, 512)] = wout_ref[:, lanes(c * 512, 512)]
    loads[2].wait()

    def norm_rows(b, core):
        @pl.loop(0, 4)
        def _(step):
            rows = rows_at(core * 128 + step * 32, 32)
            normed = normed_of(ens[b, rows, :].astype(f32))[0].astype(bf16)
            for block in range(8):
                nrm[b, rows, pl.ds(spot(block) * 128, 128)] = normed[:, block * 128 : (block + 1) * 128]

    norm_rows(1, c)
    loads[3].wait()
    place.await_all()
    gi = Gather(place, w_all, sems)
    gi.start()
    ens_own = remote(ens.at[1, mine], ens.at[1, mine], sems.take(), sems.take(), place.sibling())
    position = place.goff(0)[1] * 64 - 64 + lax.broadcasted_iota(jnp.int32, (192, 256), 0)
    starts_here = jnp.concatenate([start_ref[...]] * 4, axis=1)
    ends_here = jnp.concatenate([end_ref[...]] * 4, axis=1)
    valid = (position >= starts_here) & (position < ends_here)
    mask[...] = valid.astype(f32)
    gi.z_step(1)
    gi.x_step(0)
    gi.z_step(2)
    gi.x_step(1)
    gi.far_step(0)
    gi.z_step(3)
    halo = [
        remote(ens.at[1, mine], ens.at[0, mine], sems.take(), sems.take(), place.goff(1)),
        remote(ens.at[1, mine], ens.at[2, mine], sems.take(), sems.take(), place.goff(-1)),
    ]
    gi.x_step(2)
    gi.far_step(1)
    ens_own.wait()
    norm_rows(1, 1 - c)
    gi.z_step(4)
    gi.x_step(3)
    gi.far_step(2)

    gi.x_step(4)
    gi.far_step(3)
    gi.far_step(4)
    half_one, half_two = lanes(yl * 512, 512), lanes((1 - yl) * 512, 512)

    def first_half(b):
        @pl.loop(0, 4)
        def _(j):
            acc_kv[b, :, lanes(j * 256, 256)] = dot(nrm[b, :, half_one], w_all[half_one, lanes(512 + j * 256, 256)], NN)

    first_half(1)

    @pl.loop(0, 2)
    def _(j):
        cols = lanes(j * 256, 256)
        acc_q[:, cols] = dot(nrm[1, :, half_one], w_all[half_one, cols], NN)

    for copy in halo:
        copy.wait_recv()
    onward = [
        remote(ens.at[b, mine], ens.at[b, mine], sems.take(), sems.take(), place.sibling()) for b in (0, 2)
    ]
    norm_rows(0, c)
    norm_rows(2, c)
    for copy in onward:
        copy.wait()
    for copy in halo:
        copy.wait_send()
    norm_rows(0, 1 - c)
    norm_rows(2, 1 - c)

    @pl.loop(0, 2)
    def _(t):
        first_half(2 * t)

    gi.finish()

    @pl.loop(0, 4)
    def _(j):
        cols = lanes(512 + j * 256, 256)
        to = lanes(j * 256, 256)
        for b in range(3):
            done = (acc_kv[b, :, to] + dot(nrm[b, :, half_two], w_all[half_two, cols], NN)).astype(bf16)
            for m in range(4):
                kv[m, pl.ds(b * 64, 64), to] = done[m * 64 : (m + 1) * 64]

    @pl.loop(0, 2)
    def _(j):
        cols = lanes(j * 256, 256)
        done = (acc_q[:, cols] + dot(nrm[1, :, half_two], w_all[half_two, cols], NN)).astype(bf16)
        q[:, cols] = (done.astype(f32) * 0.125).astype(bf16)

    masks = head_masks()
    att_send, att_recv = sems.run(8), sems.run(8)

    @pl.loop(0, 4)
    def _(m):
        rows = rows_at(m * 64, 64)
        for grp in range(2):
            cols = pl.ds(grp * 256, 256)
            q4 = spread_heads(q[rows, cols], masks)
            scores = dot(kv[m, :, pl.ds(grp * 512, 256)], q4, NT)
            scores = jnp.where(mask[...] > 0.5, scores, masked_score)
            raised = jnp.exp(scores - jnp.max(scores, axis=0, keepdims=True))
            weights = raised * (1.0 / jnp.sum(raised, axis=0, keepdims=True))
            probs[m * 2 + grp] = weights
            mixed = dot(weights.astype(bf16), kv[m, :, pl.ds(grp * 512 + 256, 256)], TN)
            to = lanes(grp * 512 + c * 256, 256)
            att[rows, to] = fold_heads(mixed, masks).astype(bf16)
            remote(att.at[rows, to], att.at[rows, to], att_send(m * 2 + grp), att_recv(m * 2 + grp), place.sibling())


    def await_att(sem, col):
        @pl.loop(0, 4)
        def _(m):
            for grp in range(2):
                await_bytes(att.at[rows_at(m * 64, 64), lanes(grp * 512 + col * 256, 256)], sem(m * 2 + grp))

    await_att(att_recv, 1 - c)
    out_send, out_recv = sems.run(2), sems.run(2)

    @pl.loop(0, 2)
    def _(j):
        cols = lanes(j * 256, 256)
        done = ens[1, :, lanes(c * 512 + j * 256, 256)].astype(f32) + dot(att[...], w_all[:, lanes(1536 + j * 256, 256)], NN)
        outs[0, :, cols] = done.astype(bf16)
        remote(outs.at[0, :, cols], outs.at[1, :, cols], out_send(j), out_recv(j), place.yoff(2))

    @pl.loop(0, 8)
    def _(j):
        rows = rows_at(j * 128, 128)
        cols = lanes(j * 128, 128)
        att_t[rows, :] = att[:, cols].T
        for b in range(3):
            nrm_t[rows, pl.ds(b * 256, 256)] = nrm[b, :, cols].T

    coef = (1.0 - (1.0 - fair_alpha) / 8) / 7
    @pl.loop(0, 2)
    def _(j):
        cols = lanes(j * 256, 256)
        await_bytes(outs.at[1, :, cols], out_recv(j))

        @pl.loop(0, 4)
        def _(step):
            row = step * 16
            near = [outs[0, rows_at(m * 64 + row, 16), cols].astype(f32) for m in range(4)]
            far = [outs[1, rows_at(m * 64 + row, 16), cols].astype(f32) for m in range(4)]
            target = target_ref[rows_at(row, 16), lanes(c * 512 + j * 256, 256)].astype(f32)
            spread = [None] * 4
            for m in range(4):
                for n in range(m + 1, 4):
                    term = slope(near[m] - near[n])
                    spread[m] = term if spread[m] is None else spread[m] + term
                    spread[n] = -term if spread[n] is None else spread[n] - term
            for m in range(4):
                for n in range(4):
                    spread[m] = spread[m] + slope(near[m] - far[n])
                cot[rows_at(m * 64 + row, 16), cols] = (slope(near[m] - target) - coef * spread[m]).astype(bf16)


    ga_out, ga_in = sems.run(2), sems.run(2)

    @pl.loop(0, 4)
    def _(t):
        grp = t % 2
        cols = lanes(grp * 256, 256)
        side = jnp.where(t < 2, 1 - c, c)
        part = dot(cot[...], w_all[rows_at(grp * 512 + side * 256, 256), pl.ds(1536, 512)], NT)
        ga_part[t // 2, :, cols] = part

        @pl.when(t < 2)
        def _():
            remote(ga_part.at[0, :, cols], ga_recv.at[:, cols], ga_out(grp), ga_in(grp), place.sibling())

    to = lanes(c * 512, 512)
    cot_full[:, to] = cot[mine, :]
    cot_copy = remote(cot.at[theirs], cot_full.at[:, to], sems.take(), sems.take(), place.sibling())

    @pl.loop(0, 2)
    def _(grp):
        cols = lanes(grp * 256, 256)
        await_bytes(ga_recv.at[:, cols], ga_in(grp))
        ga[:, cols] = (ga_part[1, :, cols] + ga_recv[:, cols]).astype(bf16)

    pieces = [
        (ScatterX if i in X_FIRST else Scatter)(place, *stages[i * 5 : i * 5 + 5], sems) for i in range(len(PIECES))
    ]
    so, s0, v0, sa, v1 = pieces
    other_rows, mine_rows = (1 - yl) * 512, yl * 512
    mid = pl.ds(256, 256)

    def outer(piece, first, terms, parts=2):
        @pl.loop(0, parts)
        def _(i):
            rows = rows_at(first + i * 256, 256)
            for t, (left, inner, right, start) in enumerate(terms):
                piece.part[rows, pl.ds(t * 256, 256)] = dot(
                    left[rows, inner], right[:, pl.ds(start, 256)], NN
                ).astype(bf16)

    every = pl.ds(0, 768)
    all_o = [(att_t, pl.ds(0, 256), cot, 0), (att_t, pl.ds(0, 256), cot, 256)]
    all_q = [(nrm_t, mid, gq, 0), (nrm_t, mid, gq, 256)]
    all_kv = [(nrm_t, every, gkv, t * 256) for t in range(4)]
    all_0 = [all_q[0], all_kv[0]]
    all_a = [all_q[1], all_kv[2]]
    outer(so, other_rows, all_o)
    so.y_start()
    halos = []

    def back(grp):
        cols = pl.ds(grp * 256, 256)
        kcols = pl.ds(grp * 512, 256)
        vcols = pl.ds(grp * 512 + 256, 256)

        @pl.loop(0, 4)
        def _(m):
            rows = rows_at(m * 64, 64)
            q4 = spread_heads(q[rows, cols], masks)
            g4 = spread_heads(ga[rows, cols], masks)
            keys = kv[m, :, kcols]
            weights = probs[m * 2 + grp]
            grad = dot(kv[m, :, vcols], g4, NT)
            inner = jnp.sum(weights * grad, axis=0, keepdims=True)
            grad_scores = (weights * (grad - inner)).astype(bf16)
            for at, value in (
                (vcols, dot(weights.astype(bf16), g4, NN)), (kcols, dot(grad_scores, q4, NN))
            ):
                own_kv[rows, at] = value[64:128]
                rounded = value.astype(bf16)
                for b in range(3):
                    gkv[rows_at(b * 256 + m * 64, 64), at] = rounded[b * 64 : (b + 1) * 64]
            gq[rows, cols] = (fold_heads(dot(grad_scores, keys, TN), masks) * 0.125).astype(bf16)

    def send_halo(grp):
        at = pl.ds(grp * 512, 512)
        halos.append(
            [
                remote(gkv.at[pl.ds(0, 256), at], h_recv.at[0, :, at], sems.take(), sems.take(), place.goff(-1)),
                remote(gkv.at[pl.ds(512, 256), at], h_recv.at[1, :, at], sems.take(), sems.take(), place.goff(1)),
            ]
        )

    back(0)
    outer(s0, other_rows, all_0)
    s0.y_start()
    send_halo(0)
    outer(v0, 0, [all_kv[1]], 4)
    v0.x_one()
    outer(so, mine_rows, all_o)
    so.x_one()
    back(1)
    outer(sa, other_rows, all_a)
    sa.y_start()
    outer(v1, 0, [all_kv[3]], 4)
    v1.x_one()
    send_halo(1)
    outer(s0, mine_rows, all_0)
    v0.x_two()
    so.z_start()
    outer(sa, mine_rows, all_a)
    s0.x_one()
    v1.x_two()
    @pl.loop(0, 4)
    def _(j):
        rows = rows_at(j * 256, 256)
        gn[:, lanes(j * 256, 256)] = dot(gq[...], w_all[rows, pl.ds(0, 512)], NT)

    pair_copies = {}
    starts = [0]
    for blocks in PIECES:
        starts.append(starts[-1] + len(blocks) * 128)

    def settle(i):
        at = pl.ds(starts[i], starts[i + 1] - starts[i])
        pair[0, :, at] = pieces[i].total().astype(bf16)
        pair_copies[i] = [
            remote(pair.at[0, :, at], pair.at[slot, :, at], sems.take(), sems.take(), device)
            for slot, device in ((3, place.far_sibling()), (1, place.yoff(2)), (2, place.sibling()))
        ]

    def deliver(i):
        for copy in pair_copies[i]:
            copy.wait_recv()
        for side, slot in ((c, 0), (1 - c, 2)):
            for t, (sec, p) in enumerate(PIECES[i]):
                at = pl.ds(starts[i] + t * 128, 128)
                value = (pair[slot, :, at].astype(f32) + pair[slot + 1, :, at].astype(f32)) * factor
                if sec == 3:
                    gwout_ref[:, lanes(side * 512 + p * 128, 128)] = value
                else:
                    gwin_ref[:, lanes(sec * 1024 + side * 512 + p * 128, 128)] = value

    v0.y_start()
    settle(0)
    sa.x_one()
    v1.y_start()
    s0.z_start()
    v0.z_start()
    for pair_halo in halos:
        for copy in pair_halo:
            copy.wait()
    for grp in range(2):
        @pl.loop(0, 4)
        def _(m):
            rows = rows_at(m * 64, 64)
            at = pl.ds(grp * 512, 512)
            gkv[rows_at(256 + m * 64, 64), at] = (
                own_kv[rows, at] + h_recv[0, rows, at].astype(f32) + h_recv[1, rows, at].astype(f32)
            ).astype(bf16)

    @pl.loop(0, 4)
    def _(j):
        rows = rows_at(j * 256, 256)
        cols = lanes(j * 256, 256)
        gn[:, cols] = gn[:, cols] + dot(gkv[pl.ds(256, 256), :], w_all[rows, pl.ds(512, 1024)], NT)

    gn_copy = remote(gn.at[theirs], gn_recv, sems.take(), sems.take(), place.sibling())
    v1.z_start()
    sa.z_start()
    settle(1)
    settle(2)
    deliver(0)
    gn_copy.wait_recv()
    cot_copy.wait_recv()

    @pl.loop(0, 8)
    def _(step):
        rows = rows_at(step * 16, 16)
        normed, inverse = normed_of(ens[1, rows_at(c * 128 + step * 16, 16), :].astype(f32))
        summed = gn[rows_at(c * 128 + step * 16, 16), :] + gn_recv[rows, :]
        grad = jnp.concatenate([summed[:, spot(b) * 128 : (spot(b) + 1) * 128] for b in range(8)], axis=1)
        first = jnp.mean(grad, axis=-1, keepdims=True)
        second = jnp.mean(grad * normed, axis=-1, keepdims=True)
        gin_ref[rows, :] = (
            cot_full[rows, :].astype(f32) + inverse * (grad - first - normed * second)
        ).astype(bf16)

    settle(4)
    settle(3)
    for i in (1, 2, 4, 3):
        deliver(i)
    for copy in [gn_copy, cot_copy] + sum(pair_copies.values(), []):
        copy.wait_send()
    for j in range(2):
        cols = pl.ds(j * 256, 256)
        await_bytes(outs.at[0, :, cols], out_send(j))
        await_bytes(ga_part.at[0, :, cols], ga_out(j))
    await_att(att_send, c)
    for piece in pieces:
        piece.finish()
    assert sems.used <= SEMS


def local(ensemble, target_field, weight_in, weight_out, window_start, window_end):
    mem_dev, points, width = ensemble.shape
    bf16, f32 = jnp.bfloat16, jnp.float32
    count = mem_dev * lax.axis_size("member") * points * lax.axis_size("grid")
    vmem = pl.BlockSpec(memory_space=pltpu.VMEM)
    stages = [
        pltpu.VMEM(shape + (len(blocks) * 128,), bf16)
        for i, blocks in enumerate(PIECES)
        for shape in (
            ((1024,), (128,), (256,), (2, 256), (8, 16)) if i in X_FIRST else ((1024,), (512,), (16,), (3, 128), (8, 16))
        )
    ]

    grad_input, grad_in, grad_out = pl.pallas_call(
        functools.partial(whole_kernel, 1.0 / math.sqrt(count)),
        name="k_whole",
        out_shape=[
            jax.ShapeDtypeStruct((mem_dev * points, width), bf16),
            jax.ShapeDtypeStruct(weight_in.shape, f32),
            jax.ShapeDtypeStruct(weight_out.shape, f32),
        ],
        in_specs=[pl.BlockSpec(memory_space=pl.ANY)] * 4 + [vmem] * 2,
        out_specs=[vmem] * 3,
        scratch_shapes=[
            pltpu.VMEM((points, width), bf16),
            pltpu.VMEM((16, 3072), bf16),
            pltpu.VMEM((16, 1024), bf16),
            pltpu.VMEM((1024, 2048), bf16),
            pltpu.VMEM((3, 256, 1024), bf16),
            pltpu.VMEM((3, 256, 1024), bf16),
            pltpu.VMEM((1024, 768), bf16),
            pltpu.VMEM((256, 512), bf16),
            pltpu.VMEM((4, 192, 1024), bf16),
            pltpu.VMEM((256, 512), f32),
            pltpu.VMEM((3, 256, 1024), f32),
            pltpu.VMEM((192, 256), f32),
            pltpu.VMEM((8, 192, 256), f32),
            pltpu.VMEM((256, 1024), bf16),
            pltpu.VMEM((1024, 256), bf16),
            pltpu.VMEM((2, 256, 512), bf16),
            pltpu.VMEM((256, 512), bf16),
            pltpu.VMEM((128, 1024), bf16),
            pltpu.VMEM((2, 256, 512), f32),
            pltpu.VMEM((256, 512), f32),
            pltpu.VMEM((256, 512), bf16),
            pltpu.VMEM((256, 512), bf16),
            pltpu.VMEM((256, 1024), f32),
            pltpu.VMEM((768, 1024), bf16),
            pltpu.VMEM((2, 256, 1024), bf16),
            pltpu.VMEM((256, 1024), f32),
            pltpu.VMEM((128, 1024), f32),
        ]
        + stages
        + [
            pltpu.VMEM((4, 16, 2048), bf16),
            pltpu.SemaphoreType.DMA((SEMS,)),
        ],
        compiler_params=pltpu.CompilerParams(
            collective_id=1, has_side_effects=True, vmem_limit_bytes=56 << 20
        ),
    )(ensemble.reshape(mem_dev * points, width), target_field, weight_in, weight_out,
      window_start.reshape(1, points), window_end.reshape(1, points))
    return grad_input.reshape(ensemble.shape), grad_in, grad_out


norm_eps = 1e-05
smooth_width = 0.1
fair_alpha = 0.95
masked_score = -1e30


def solution(mesh):
    in_specs = (
        P("member", "grid", None),
        P("grid", None),
        P("grid", None),
        P("grid", None),
        P("grid"),
        P("grid"),
    )
    out_specs = (P("member", "grid", None), P("grid", None), P("grid", None))
    return jax.shard_map(local, mesh=mesh, in_specs=in_specs, out_specs=out_specs, check_vma=False)
```

```python
import functools
import math

import jax
import jax.numpy as jnp
from jax import lax
from jax.experimental import pallas as pl
from jax.experimental.pallas import tpu as pltpu
from jax.sharding import PartitionSpec as P

MESH = pl.DeviceIdType.MESH


class Place:
    def __init__(self):
        g = lax.axis_index("grid")
        m = lax.axis_index("member")
        self.x, self.yl, self.z = g // 16, (g // 8) % 2, g % 8
        self.yh, self.c = m // 2, m % 2

    def dev(self, x, yl, z, yh, c):
        return (yh * 2 + c, (x * 2 + yl) * 8 + z)

    def zoff(self, s):
        return self.dev(self.x, self.yl, (self.z + s + 8) % 8, self.yh, self.c)

    def xoff(self, s):
        return self.dev((self.x + s + 4) % 4, self.yl, self.z, self.yh, self.c)

    def yoff(self, s):
        y = (2 * self.yh + self.yl + s + 4) % 4
        return self.dev(self.x, y % 2, self.z, y // 2, self.c)

    def sibling(self):
        return self.dev(self.x, self.yl, self.z, self.yh, 1 - self.c)

    def goff(self, s):
        g = ((self.x * 2 + self.yl) * 8 + self.z + s + 64) % 64
        return (self.yh * 2 + self.c, g)

    def far_sibling(self):
        return self.dev(self.x, self.yl, self.z, 1 - self.yh, 1 - self.c)

    def partners(self):
        return (
            [self.zoff(s) for s in range(1, 8)]
            + [self.xoff(s) for s in (1, -1, 2)]
            + [self.yoff(s) for s in (1, -1, 2)]
            + [self.sibling(), self.far_sibling(), self.goff(1), self.goff(-1)]
        )

    def signal(self):
        barrier = pltpu.get_barrier_semaphore()
        for partner in self.partners():
            pl.semaphore_signal(barrier, 1, device_id=partner, device_id_type=MESH)

    def await_all(self):
        pl.semaphore_wait(pltpu.get_barrier_semaphore(), len(self.partners()))


def remote(src, dst, send, recv, device):
    copy = pltpu.make_async_remote_copy(
        src_ref=src, dst_ref=dst, send_sem=send, recv_sem=recv, device_id=device, device_id_type=MESH
    )
    copy.start()
    return copy


def await_bytes(ref, sem):
    pltpu.make_async_copy(ref, ref, sem).wait()


def rows_at(start, count, unit=16):
    return pl.ds(pl.multiple_of(start, unit), count)


def lanes(start, count):
    return pl.ds(pl.multiple_of(start, 128), count)


def dot(a, b, dims):
    return lax.dot_general(a, b, (dims, ((), ())), preferred_element_type=jnp.float32)


NN = ((1,), (0,))
NT = ((1,), (1,))
TN = ((0,), (0,))


class Sems:
    def __init__(self, array):
        self.array, self.used = array, 0

    def take(self, count=None):
        start = self.used
        self.used += 1 if count is None else count
        if count is None:
            return self.array.at[start]
        return [self.array.at[start + i] for i in range(count)]

    def run(self, count):
        start = self.used
        self.used += count
        return lambda i: self.array.at[start + i]


def side_of(s):
    return 0 if s in (0, 1, 2, 3) else 1


class Gather:
    def __init__(self, place, buf, sems):
        self.place, self.buf, self.cols = place, buf, buf.shape[1]
        self.z_send, self.z_recv = sems.take(8), sems.take(8)
        self.x_send, self.x_recv, self.x_far = sems.take(2), [sems.take(8), sems.take(8)], sems.take(8)
        self.y_send, self.y_recv = sems.take(2), sems.take(2)
        self.z_copies = []

    def shard(self, xs, s):
        place = self.place
        start = place.yl * 512 + ((place.x + xs + 4) % 4) * 128 + ((place.z + s + 8) % 8) * 16
        return self.buf.at[rows_at(start, 16)]

    def to_y(self, ref, s):
        side = side_of(s)
        remote(ref, ref, self.y_send[side], self.y_recv[side], self.place.yoff(1 - 2 * side))

    def pass_on(self, s):
        ref, place = self.shard(0, s), self.place
        for way, sign in ((0, 1), (1, -1)):
            remote(ref, ref, self.x_send[way], self.x_recv[way][s % 8], place.xoff(sign))
        self.to_y(ref, s)

    def start(self):
        ref = self.shard(0, 0)
        for s in (1, -1, 2, -2, 3, -3, 4):
            self.z_copies.append(remote(ref, ref, self.z_send[s % 8], self.z_recv[-s % 8], self.place.zoff(s)))
        self.pass_on(0)

    def z_step(self, step):
        for s in sorted({-step, step} - {-4}):
            await_bytes(self.shard(0, s), self.z_recv[s % 8])
            self.pass_on(s)

    def x_step(self, step):
        for s in sorted({-step, step} - {-4}):
            for way, sign in ((0, 1), (1, -1)):
                ref = self.shard(-sign, s)
                await_bytes(ref, self.x_recv[way][s % 8])
                if side_of(s) == way:
                    remote(ref, ref, self.x_send[way], self.x_far[s % 8], self.place.xoff(sign))
                self.to_y(ref, s)

    def far_step(self, step):
        for s in sorted({-step, step} - {-4}):
            ref = self.shard(2, s)
            await_bytes(ref, self.x_far[s % 8])
            self.to_y(ref, s)

    def finish(self):
        for copy in self.z_copies:
            copy.wait_send()
        for side in range(2):
            await_bytes(self.buf.at[pl.ds(0, 256)], self.y_recv[side])
            await_bytes(self.buf.at[pl.ds(0, 192)], self.x_send[side])
            await_bytes(self.buf.at[pl.ds(0, 256)], self.y_send[side])


def add_rows(dst, start, count, *sources):
    @pl.loop(0, count // 32)
    def _(step):
        rows = rows_at(start + step * 32, 32)
        total = dst[rows, :].astype(jnp.float32)
        for ref, first in sources:
            total = total + ref[rows_at(first + step * 32, 32), :].astype(jnp.float32)
        dst[rows, :] = total.astype(dst.dtype)


class Scatter:
    def __init__(self, place, part, y_stage, x_stage, x_last, z_stage, sems):
        self.place, self.part, self.y_stage = place, part, y_stage
        self.x_stage, self.x_last, self.z_stage = x_stage, x_last, z_stage
        self.y_send, self.y_recv = sems.take(2), [sems.run(4), sems.run(4)]
        self.x_send, self.x_recv = sems.take(4), sems.take(4)
        self.z_send, self.z_recv = sems.run(8), sems.run(8)
        self.mine, self.other = place.yl * 512, (1 - place.yl) * 512

    def block(self, xs):
        return ((self.place.x + xs + 4) % 4) * 128

    def y_start(self):
        @pl.loop(0, 4)
        def _(index):
            start = self.block(jnp.where(index == 2, 3, jnp.where(index == 3, 0, 2 - index)))
            for side, sign in ((0, 1), (1, -1)):
                at = start + side * 64
                remote(
                    self.part.at[rows_at(self.other + at, 64)], self.y_stage.at[rows_at(at, 64)],
                    self.y_send[side], self.y_recv[side](index), self.place.yoff(sign),
                )

    def take_y(self, index, xs):
        start = self.block(xs)
        for side in range(2):
            await_bytes(self.y_stage.at[rows_at(start + side * 64, 64)], self.y_recv[side](index))
        add_rows(self.part, self.mine + start, 128, (self.y_stage, start))

    def x_one(self):
        for index, xs in enumerate((2, 1, -1)):
            self.take_y(index, xs)
            remote(self.part.at[rows_at(self.mine + self.block(xs), 128)], self.x_last.at[index],
                   self.x_send[index], self.x_recv[index], self.place.xoff(xs))

    def row(self, s):
        return rows_at(self.mine + self.block(0) + ((self.place.z + s) % 8) * 16, 16)

    def z_start(self):
        self.take_y(3, 0)
        for index in range(3):
            await_bytes(self.x_last.at[index], self.x_recv[index])
        add_rows(self.part, self.mine + self.block(0), 128, *[(self.x_last.at[index], 0) for index in range(3)])
        self.z_out()

    def z_out(self):
        @pl.loop(1, 8)
        def _(s):
            remote(self.part.at[self.row(s)], self.z_stage.at[s], self.z_send(s), self.z_recv(s), self.place.zoff(s))

    def z_drain(self):
        @pl.loop(1, 8)
        def _(s):
            await_bytes(self.part.at[pl.ds(0, 16)], self.z_send(s))

    def total(self):
        @pl.loop(1, 8)
        def _(s):
            await_bytes(self.z_stage.at[s], self.z_recv(s))

        total = self.part[self.row(0), :].astype(jnp.float32)
        for s in range(1, 8):
            total = total + self.z_stage[s].astype(jnp.float32)
        return total

    def finish(self):
        self.z_drain()
        for index in range(3):
            await_bytes(self.part.at[pl.ds(0, 128)], self.x_send[index])
        for side in range(2):
            await_bytes(self.part.at[pl.ds(0, 256)], self.y_send[side])


SEMS = 312
class ScatterX(Scatter):
    def x_one(self):
        for way, sign in ((0, 1), (1, -1)):
            remote(self.part.at[rows_at(way * 512 + self.block(2), 128)], self.x_stage.at[pl.ds(way * 128, 128)],
                   self.x_send[way], self.x_recv[way], self.place.xoff(sign))

    def x_two(self):
        for way, sign in ((0, 1), (1, -1)):
            await_bytes(self.x_stage.at[pl.ds(way * 128, 128)], self.x_recv[way])
            add_rows(self.part, way * 512 + self.block(sign), 128, (self.x_stage, way * 128))
            for yl in range(2):
                remote(self.part.at[rows_at(yl * 512 + self.block(sign), 128)],
                       self.x_last.at[way, pl.ds(yl * 128, 128)],
                       self.x_send[2 + way], self.x_recv[2 + way], self.place.xoff(sign))

    def y_start(self):
        for way in range(2):
            await_bytes(self.x_last.at[way], self.x_recv[2 + way])
        for yl in range(2):
            last = [(self.x_last.at[way], yl * 128) for way in range(2)]
            add_rows(self.part, yl * 512 + self.block(0), 128, *last)
        for side, sign in ((0, 1), (1, -1)):
            remote(self.part.at[rows_at(self.other + self.block(0) + side * 64, 64)],
                   self.y_stage.at[pl.ds(side * 64, 64)],
                   self.y_send[side], self.y_recv[side](0), self.place.yoff(sign))

    def z_start(self):
        for side in range(2):
            await_bytes(self.y_stage.at[pl.ds(side * 64, 64)], self.y_recv[side](0))
        add_rows(self.part, self.mine + self.block(0), 128, (self.y_stage, 0))
        self.z_out()

    def finish(self):
        self.z_drain()
        for way in range(2):
            await_bytes(self.part.at[pl.ds(0, 128)], self.x_send[way])
            await_bytes(self.part.at[pl.ds(0, 256)], self.x_send[2 + way])
            await_bytes(self.part.at[pl.ds(0, 64)], self.y_send[way])


GROUPS = ((0, 2), (1, 3))
LOCAL = [(0, p) for group in GROUPS for p in group] + [
    (sec, p) for group in GROUPS for sec in (1, 2) for p in group
]
PIECES = (
    [(3, p) for p in range(4)],
    [(sec, p) for sec in range(2) for p in GROUPS[0]],
    [(2, p) for p in GROUPS[0]],
    [(sec, p) for sec in range(2) for p in GROUPS[1]],
    [(2, p) for p in GROUPS[1]],
)
X_FIRST = (2, 4)


def spot(block):
    return (block % 2) * 4 + block // 2


def normed_of(wide):
    center = wide - jnp.mean(wide, axis=-1, keepdims=True)
    inverse = lax.rsqrt(jnp.mean(center * center, axis=-1, keepdims=True) + norm_eps)
    return center * inverse, inverse


def slope(delta):
    return delta * lax.rsqrt(delta * delta + smooth_width * smooth_width)


def head_masks():
    lane = lax.broadcasted_iota(jnp.int32, (64, 256), 1) // 64
    return [(lane == h).astype(jnp.float32) for h in range(4)]


def spread_heads(block, masks):
    wide = block.astype(jnp.float32)
    return jnp.concatenate([(wide * mask).astype(jnp.bfloat16) for mask in masks], axis=0)


def fold_heads(wide, masks):
    total = wide[0:64] * masks[0]
    for h in range(1, 4):
        total = total + wide[h * 64 : (h + 1) * 64] * masks[h]
    return total


def whole_kernel(
    factor, ens_hbm, target_hbm, win_hbm, wout_hbm, start_ref, end_ref, gin_ref, gwin_ref, gwout_ref,
    target_ref, win_ref, wout_ref,
    w_all, ens, nrm, nrm_t, q, kv, acc_q, acc_kv, mask, probs, att, att_t, outs, cot, cot_full,
    ga_part, ga_recv, ga, gq, own_kv, gkv, h_recv, gn, gn_recv, *rest,
):
    *stages, pair, sem_array = rest
    place = Place()
    sems = Sems(sem_array)
    c, yl = place.c, place.yl
    own = yl * 512 + place.x * 128 + place.z * 16
    bf16, f32 = jnp.bfloat16, jnp.float32
    place.signal()
    mine = rows_at(c * 128, 128)
    theirs = rows_at((1 - c) * 128, 128)
    loads = [
        pltpu.make_async_copy(src, dst, sems.take())
        for src, dst in (
            (win_hbm, win_ref), (wout_hbm, wout_ref), (ens_hbm, ens.at[1, mine]), (target_hbm, target_ref)
        )
    ]
    for load in loads:
        load.start()
    for load in loads[:2]:
        load.wait()
    for t, (sec, p) in enumerate(LOCAL):
        w_all[rows_at(own, 16), pl.ds(t * 128, 128)] = win_ref[:, lanes(sec * 1024 + c * 512 + p * 128, 128)]
    w_all[rows_at(own, 16), pl.ds(1536, 512)] = wout_ref[:, lanes(c * 512, 512)]
    loads[2].wait()

    def norm_rows(b, core):
        @pl.loop(0, 4)
        def _(step):
            rows = rows_at(core * 128 + step * 32, 32)
            normed = normed_of(ens[b, rows, :].astype(f32))[0].astype(bf16)
            for block in range(8):
                nrm[b, rows, pl.ds(spot(block) * 128, 128)] = normed[:, block * 128 : (block + 1) * 128]

    norm_rows(1, c)
    loads[3].wait()
    place.await_all()
    gi = Gather(place, w_all, sems)
    gi.start()
    ens_own = remote(ens.at[1, mine], ens.at[1, mine], sems.take(), sems.take(), place.sibling())
    position = place.goff(0)[1] * 64 - 64 + lax.broadcasted_iota(jnp.int32, (192, 256), 0)
    starts_here = jnp.concatenate([start_ref[...]] * 4, axis=1)
    ends_here = jnp.concatenate([end_ref[...]] * 4, axis=1)
    valid = (position >= starts_here) & (position < ends_here)
    mask[...] = valid.astype(f32)
    gi.z_step(1)
    gi.x_step(0)
    gi.z_step(2)
    gi.x_step(1)
    gi.far_step(0)
    gi.z_step(3)
    halo = [
        remote(ens.at[1, mine], ens.at[0, mine], sems.take(), sems.take(), place.goff(1)),
        remote(ens.at[1, mine], ens.at[2, mine], sems.take(), sems.take(), place.goff(-1)),
    ]
    gi.x_step(2)
    gi.far_step(1)
    ens_own.wait()
    norm_rows(1, 1 - c)
    gi.z_step(4)
    gi.x_step(3)
    gi.far_step(2)

    gi.x_step(4)
    gi.far_step(3)
    gi.far_step(4)
    half_one, half_two = lanes(yl * 512, 512), lanes((1 - yl) * 512, 512)

    def first_half(b):
        @pl.loop(0, 4)
        def _(j):
            acc_kv[b, :, lanes(j * 256, 256)] = dot(nrm[b, :, half_one], w_all[half_one, lanes(512 + j * 256, 256)], NN)

    first_half(1)

    @pl.loop(0, 2)
    def _(j):
        cols = lanes(j * 256, 256)
        acc_q[:, cols] = dot(nrm[1, :, half_one], w_all[half_one, cols], NN)

    for copy in halo:
        copy.wait_recv()
    onward = [
        remote(ens.at[b, mine], ens.at[b, mine], sems.take(), sems.take(), place.sibling()) for b in (0, 2)
    ]
    norm_rows(0, c)
    norm_rows(2, c)
    for copy in onward:
        copy.wait()
    for copy in halo:
        copy.wait_send()
    norm_rows(0, 1 - c)
    norm_rows(2, 1 - c)

    @pl.loop(0, 2)
    def _(t):
        first_half(2 * t)

    gi.finish()

    @pl.loop(0, 4)
    def _(j):
        cols = lanes(512 + j * 256, 256)
        to = lanes(j * 256, 256)
        for b in range(3):
            done = (acc_kv[b, :, to] + dot(nrm[b, :, half_two], w_all[half_two, cols], NN)).astype(bf16)
            for m in range(4):
                kv[m, pl.ds(b * 64, 64), to] = done[m * 64 : (m + 1) * 64]

    @pl.loop(0, 2)
    def _(j):
        cols = lanes(j * 256, 256)
        done = (acc_q[:, cols] + dot(nrm[1, :, half_two], w_all[half_two, cols], NN)).astype(bf16)
        q[:, cols] = (done.astype(f32) * 0.125).astype(bf16)

    masks = head_masks()
    att_send, att_recv = sems.run(8), sems.run(8)

    @pl.loop(0, 4)
    def _(m):
        rows = rows_at(m * 64, 64)
        for grp in range(2):
            cols = pl.ds(grp * 256, 256)
            q4 = spread_heads(q[rows, cols], masks)
            scores = dot(kv[m, :, pl.ds(grp * 512, 256)], q4, NT)
            scores = jnp.where(mask[...] > 0.5, scores, masked_score)
            raised = jnp.exp(scores - jnp.max(scores, axis=0, keepdims=True))
            weights = raised * (1.0 / jnp.sum(raised, axis=0, keepdims=True))
            probs[m * 2 + grp] = weights
            mixed = dot(weights.astype(bf16), kv[m, :, pl.ds(grp * 512 + 256, 256)], TN)
            to = lanes(grp * 512 + c * 256, 256)
            att[rows, to] = fold_heads(mixed, masks).astype(bf16)
            remote(att.at[rows, to], att.at[rows, to], att_send(m * 2 + grp), att_recv(m * 2 + grp), place.sibling())


    def await_att(sem, col):
        @pl.loop(0, 4)
        def _(m):
            for grp in range(2):
                await_bytes(att.at[rows_at(m * 64, 64), lanes(grp * 512 + col * 256, 256)], sem(m * 2 + grp))

    await_att(att_recv, 1 - c)
    out_send, out_recv = sems.run(2), sems.run(2)

    @pl.loop(0, 2)
    def _(j):
        cols = lanes(j * 256, 256)
        done = ens[1, :, lanes(c * 512 + j * 256, 256)].astype(f32) + dot(att[...], w_all[:, lanes(1536 + j * 256, 256)], NN)
        outs[0, :, cols] = done.astype(bf16)
        remote(outs.at[0, :, cols], outs.at[1, :, cols], out_send(j), out_recv(j), place.yoff(2))

    @pl.loop(0, 8)
    def _(j):
        rows = rows_at(j * 128, 128)
        cols = lanes(j * 128, 128)
        att_t[rows, :] = att[:, cols].T
        for b in range(3):
            nrm_t[rows, pl.ds(b * 256, 256)] = nrm[b, :, cols].T

    coef = (1.0 - (1.0 - fair_alpha) / 8) / 7
    @pl.loop(0, 2)
    def _(j):
        cols = lanes(j * 256, 256)
        await_bytes(outs.at[1, :, cols], out_recv(j))

        @pl.loop(0, 4)
        def _(step):
            row = step * 16
            near = [outs[0, rows_at(m * 64 + row, 16), cols].astype(f32) for m in range(4)]
            far = [outs[1, rows_at(m * 64 + row, 16), cols].astype(f32) for m in range(4)]
            target = target_ref[rows_at(row, 16), lanes(c * 512 + j * 256, 256)].astype(f32)
            spread = [None] * 4
            for m in range(4):
                for n in range(m + 1, 4):
                    term = slope(near[m] - near[n])
                    spread[m] = term if spread[m] is None else spread[m] + term
                    spread[n] = -term if spread[n] is None else spread[n] - term
            for m in range(4):
                for n in range(4):
                    spread[m] = spread[m] + slope(near[m] - far[n])
                cot[rows_at(m * 64 + row, 16), cols] = (slope(near[m] - target) - coef * spread[m]).astype(bf16)


    ga_out, ga_in = sems.run(2), sems.run(2)

    @pl.loop(0, 4)
    def _(t):
        grp = t % 2
        cols = lanes(grp * 256, 256)
        side = jnp.where(t < 2, 1 - c, c)
        part = dot(cot[...], w_all[rows_at(grp * 512 + side * 256, 256), pl.ds(1536, 512)], NT)
        ga_part[t // 2, :, cols] = part

        @pl.when(t < 2)
        def _():
            remote(ga_part.at[0, :, cols], ga_recv.at[:, cols], ga_out(grp), ga_in(grp), place.sibling())

    to = lanes(c * 512, 512)
    cot_full[:, to] = cot[mine, :]
    cot_copy = remote(cot.at[theirs], cot_full.at[:, to], sems.take(), sems.take(), place.sibling())

    @pl.loop(0, 2)
    def _(grp):
        cols = lanes(grp * 256, 256)
        await_bytes(ga_recv.at[:, cols], ga_in(grp))
        ga[:, cols] = (ga_part[1, :, cols] + ga_recv[:, cols]).astype(bf16)

    pieces = [
        (ScatterX if i in X_FIRST else Scatter)(place, *stages[i * 5 : i * 5 + 5], sems) for i in range(len(PIECES))
    ]
    so, s0, v0, sa, v1 = pieces
    other_rows, mine_rows = (1 - yl) * 512, yl * 512
    mid = pl.ds(256, 256)

    def outer(piece, first, terms, parts=2):
        @pl.loop(0, parts)
        def _(i):
            rows = rows_at(first + i * 256, 256)
            for t, (left, inner, right, start) in enumerate(terms):
                piece.part[rows, pl.ds(t * 256, 256)] = dot(
                    left[rows, inner], right[:, pl.ds(start, 256)], NN
                ).astype(bf16)

    every = pl.ds(0, 768)
    all_o = [(att_t, pl.ds(0, 256), cot, 0), (att_t, pl.ds(0, 256), cot, 256)]
    all_q = [(nrm_t, mid, gq, 0), (nrm_t, mid, gq, 256)]
    all_kv = [(nrm_t, every, gkv, t * 256) for t in range(4)]
    all_0 = [all_q[0], all_kv[0]]
    all_a = [all_q[1], all_kv[2]]
    outer(so, other_rows, all_o)
    so.y_start()
    halos = []

    def back(grp):
        cols = pl.ds(grp * 256, 256)
        kcols = pl.ds(grp * 512, 256)
        vcols = pl.ds(grp * 512 + 256, 256)

        @pl.loop(0, 4)
        def _(m):
            rows = rows_at(m * 64, 64)
            q4 = spread_heads(q[rows, cols], masks)
            g4 = spread_heads(ga[rows, cols], masks)
            keys = kv[m, :, kcols]
            weights = probs[m * 2 + grp]
            grad = dot(kv[m, :, vcols], g4, NT)
            inner = jnp.sum(weights * grad, axis=0, keepdims=True)
            grad_scores = (weights * (grad - inner)).astype(bf16)
            for at, value in (
                (vcols, dot(weights.astype(bf16), g4, NN)), (kcols, dot(grad_scores, q4, NN))
            ):
                own_kv[rows, at] = value[64:128]
                rounded = value.astype(bf16)
                for b in range(3):
                    gkv[rows_at(b * 256 + m * 64, 64), at] = rounded[b * 64 : (b + 1) * 64]
            gq[rows, cols] = (fold_heads(dot(grad_scores, keys, TN), masks) * 0.125).astype(bf16)

    def send_halo(grp):
        at = pl.ds(grp * 512, 512)
        halos.append(
            [
                remote(gkv.at[pl.ds(0, 256), at], h_recv.at[0, :, at], sems.take(), sems.take(), place.goff(-1)),
                remote(gkv.at[pl.ds(512, 256), at], h_recv.at[1, :, at], sems.take(), sems.take(), place.goff(1)),
            ]
        )

    back(0)
    send_halo(0)
    outer(s0, other_rows, all_0)
    s0.y_start()
    outer(v0, 0, [all_kv[1]], 4)
    v0.x_one()
    outer(so, mine_rows, all_o)
    so.x_one()
    back(1)
    send_halo(1)
    outer(sa, other_rows, all_a)
    sa.y_start()
    outer(v1, 0, [all_kv[3]], 4)
    v1.x_one()
    outer(s0, mine_rows, all_0)
    v0.x_two()
    so.z_start()
    outer(sa, mine_rows, all_a)
    s0.x_one()
    v1.x_two()
    @pl.loop(0, 4)
    def _(j):
        rows = rows_at(j * 256, 256)
        gn[:, lanes(j * 256, 256)] = dot(gq[...], w_all[rows, pl.ds(0, 512)], NT)

    pair_copies = {}
    starts = [0]
    for blocks in PIECES:
        starts.append(starts[-1] + len(blocks) * 128)

    def settle(i):
        at = pl.ds(starts[i], starts[i + 1] - starts[i])
        pair[0, :, at] = pieces[i].total().astype(bf16)
        pair_copies[i] = [
            remote(pair.at[0, :, at], pair.at[slot, :, at], sems.take(), sems.take(), device)
            for slot, device in ((3, place.far_sibling()), (1, place.yoff(2)), (2, place.sibling()))
        ]

    def deliver(i):
        for copy in pair_copies[i]:
            copy.wait_recv()
        for side, slot in ((c, 0), (1 - c, 2)):
            for t, (sec, p) in enumerate(PIECES[i]):
                at = pl.ds(starts[i] + t * 128, 128)
                value = (pair[slot, :, at].astype(f32) + pair[slot + 1, :, at].astype(f32)) * factor
                if sec == 3:
                    gwout_ref[:, lanes(side * 512 + p * 128, 128)] = value
                else:
                    gwin_ref[:, lanes(sec * 1024 + side * 512 + p * 128, 128)] = value

    v0.y_start()
    settle(0)
    sa.x_one()
    v1.y_start()
    s0.z_start()
    v0.z_start()
    for pair_halo in halos:
        for copy in pair_halo:
            copy.wait()
    for grp in range(2):
        @pl.loop(0, 4)
        def _(m):
            rows = rows_at(m * 64, 64)
            at = pl.ds(grp * 512, 512)
            gkv[rows_at(256 + m * 64, 64), at] = (
                own_kv[rows, at] + h_recv[0, rows, at].astype(f32) + h_recv[1, rows, at].astype(f32)
            ).astype(bf16)

    @pl.loop(0, 4)
    def _(j):
        rows = rows_at(j * 256, 256)
        cols = lanes(j * 256, 256)
        gn[:, cols] = gn[:, cols] + dot(gkv[pl.ds(256, 256), :], w_all[rows, pl.ds(512, 1024)], NT)

    gn_copy = remote(gn.at[theirs], gn_recv, sems.take(), sems.take(), place.sibling())
    v1.z_start()
    sa.z_start()
    settle(1)
    settle(2)
    deliver(0)
    gn_copy.wait_recv()
    cot_copy.wait_recv()

    @pl.loop(0, 8)
    def _(step):
        rows = rows_at(step * 16, 16)
        normed, inverse = normed_of(ens[1, rows_at(c * 128 + step * 16, 16), :].astype(f32))
        summed = gn[rows_at(c * 128 + step * 16, 16), :] + gn_recv[rows, :]
        grad = jnp.concatenate([summed[:, spot(b) * 128 : (spot(b) + 1) * 128] for b in range(8)], axis=1)
        first = jnp.mean(grad, axis=-1, keepdims=True)
        second = jnp.mean(grad * normed, axis=-1, keepdims=True)
        gin_ref[rows, :] = (
            cot_full[rows, :].astype(f32) + inverse * (grad - first - normed * second)
        ).astype(bf16)

    settle(4)
    settle(3)
    for i in (1, 2, 4, 3):
        deliver(i)
    for copy in [gn_copy, cot_copy] + sum(pair_copies.values(), []):
        copy.wait_send()
    for j in range(2):
        cols = pl.ds(j * 256, 256)
        await_bytes(outs.at[0, :, cols], out_send(j))
        await_bytes(ga_part.at[0, :, cols], ga_out(j))
    await_att(att_send, c)
    for piece in pieces:
        piece.finish()
    assert sems.used <= SEMS


def local(ensemble, target_field, weight_in, weight_out, window_start, window_end):
    mem_dev, points, width = ensemble.shape
    bf16, f32 = jnp.bfloat16, jnp.float32
    count = mem_dev * lax.axis_size("member") * points * lax.axis_size("grid")
    vmem = pl.BlockSpec(memory_space=pltpu.VMEM)
    stages = [
        pltpu.VMEM(shape + (len(blocks) * 128,), bf16)
        for i, blocks in enumerate(PIECES)
        for shape in (
            ((1024,), (128,), (256,), (2, 256), (8, 16)) if i in X_FIRST else ((1024,), (512,), (16,), (3, 128), (8, 16))
        )
    ]

    grad_input, grad_in, grad_out = pl.pallas_call(
        functools.partial(whole_kernel, 1.0 / math.sqrt(count)),
        name="k_whole",
        out_shape=[
            jax.ShapeDtypeStruct((mem_dev * points, width), bf16),
            jax.ShapeDtypeStruct(weight_in.shape, f32),
            jax.ShapeDtypeStruct(weight_out.shape, f32),
        ],
        in_specs=[pl.BlockSpec(memory_space=pl.ANY)] * 4 + [vmem] * 2,
        out_specs=[vmem] * 3,
        scratch_shapes=[
            pltpu.VMEM((points, width), bf16),
            pltpu.VMEM((16, 3072), bf16),
            pltpu.VMEM((16, 1024), bf16),
            pltpu.VMEM((1024, 2048), bf16),
            pltpu.VMEM((3, 256, 1024), bf16),
            pltpu.VMEM((3, 256, 1024), bf16),
            pltpu.VMEM((1024, 768), bf16),
            pltpu.VMEM((256, 512), bf16),
            pltpu.VMEM((4, 192, 1024), bf16),
            pltpu.VMEM((256, 512), f32),
            pltpu.VMEM((3, 256, 1024), f32),
            pltpu.VMEM((192, 256), f32),
            pltpu.VMEM((8, 192, 256), f32),
            pltpu.VMEM((256, 1024), bf16),
            pltpu.VMEM((1024, 256), bf16),
            pltpu.VMEM((2, 256, 512), bf16),
            pltpu.VMEM((256, 512), bf16),
            pltpu.VMEM((128, 1024), bf16),
            pltpu.VMEM((2, 256, 512), f32),
            pltpu.VMEM((256, 512), f32),
            pltpu.VMEM((256, 512), bf16),
            pltpu.VMEM((256, 512), bf16),
            pltpu.VMEM((256, 1024), f32),
            pltpu.VMEM((768, 1024), bf16),
            pltpu.VMEM((2, 256, 1024), bf16),
            pltpu.VMEM((256, 1024), f32),
            pltpu.VMEM((128, 1024), f32),
        ]
        + stages
        + [
            pltpu.VMEM((4, 16, 2048), bf16),
            pltpu.SemaphoreType.DMA((SEMS,)),
        ],
        compiler_params=pltpu.CompilerParams(
            collective_id=1, has_side_effects=True, vmem_limit_bytes=56 << 20
        ),
    )(ensemble.reshape(mem_dev * points, width), target_field, weight_in, weight_out,
      window_start.reshape(1, points), window_end.reshape(1, points))
    return grad_input.reshape(ensemble.shape), grad_in, grad_out


norm_eps = 1e-05
smooth_width = 0.1
fair_alpha = 0.95
masked_score = -1e30


def solution(mesh):
    in_specs = (
        P("member", "grid", None),
        P("grid", None),
        P("grid", None),
        P("grid", None),
        P("grid"),
        P("grid"),
    )
    out_specs = (P("member", "grid", None), P("grid", None), P("grid", None))
    return jax.shard_map(local, mesh=mesh, in_specs=in_specs, out_specs=out_specs, check_vma=False)
```

```python
import functools
import math

import jax
import jax.numpy as jnp
from jax import lax
from jax.experimental import pallas as pl
from jax.experimental.pallas import tpu as pltpu
from jax.sharding import PartitionSpec as P

MESH = pl.DeviceIdType.MESH


class Place:
    def __init__(self):
        g = lax.axis_index("grid")
        m = lax.axis_index("member")
        self.x, self.yl, self.z = g // 16, (g // 8) % 2, g % 8
        self.yh, self.c = m // 2, m % 2

    def dev(self, x, yl, z, yh, c):
        return (yh * 2 + c, (x * 2 + yl) * 8 + z)

    def zoff(self, s):
        return self.dev(self.x, self.yl, (self.z + s + 8) % 8, self.yh, self.c)

    def xoff(self, s):
        return self.dev((self.x + s + 4) % 4, self.yl, self.z, self.yh, self.c)

    def yoff(self, s):
        y = (2 * self.yh + self.yl + s + 4) % 4
        return self.dev(self.x, y % 2, self.z, y // 2, self.c)

    def sibling(self):
        return self.dev(self.x, self.yl, self.z, self.yh, 1 - self.c)

    def goff(self, s):
        g = ((self.x * 2 + self.yl) * 8 + self.z + s + 64) % 64
        return (self.yh * 2 + self.c, g)

    def far_sibling(self):
        return self.dev(self.x, self.yl, self.z, 1 - self.yh, 1 - self.c)

    def partners(self):
        return (
            [self.zoff(s) for s in range(1, 8)]
            + [self.xoff(s) for s in (1, -1, 2)]
            + [self.yoff(s) for s in (1, -1, 2)]
            + [self.sibling(), self.far_sibling(), self.goff(1), self.goff(-1)]
        )

    def signal(self):
        barrier = pltpu.get_barrier_semaphore()
        for partner in self.partners():
            pl.semaphore_signal(barrier, 1, device_id=partner, device_id_type=MESH)

    def await_all(self):
        pl.semaphore_wait(pltpu.get_barrier_semaphore(), len(self.partners()))


def remote(src, dst, send, recv, device):
    copy = pltpu.make_async_remote_copy(
        src_ref=src, dst_ref=dst, send_sem=send, recv_sem=recv, device_id=device, device_id_type=MESH
    )
    copy.start()
    return copy


def await_bytes(ref, sem):
    pltpu.make_async_copy(ref, ref, sem).wait()


def rows_at(start, count, unit=16):
    return pl.ds(pl.multiple_of(start, unit), count)


def lanes(start, count):
    return pl.ds(pl.multiple_of(start, 128), count)


def dot(a, b, dims):
    return lax.dot_general(a, b, (dims, ((), ())), preferred_element_type=jnp.float32)


NN = ((1,), (0,))
NT = ((1,), (1,))
TN = ((0,), (0,))


class Sems:
    def __init__(self, array):
        self.array, self.used = array, 0

    def take(self, count=None):
        start = self.used
        self.used += 1 if count is None else count
        if count is None:
            return self.array.at[start]
        return [self.array.at[start + i] for i in range(count)]

    def run(self, count):
        start = self.used
        self.used += count
        return lambda i: self.array.at[start + i]


def side_of(s):
    return 0 if s in (0, 1, 2, 3) else 1


class Gather:
    def __init__(self, place, buf, sems):
        self.place, self.buf, self.cols = place, buf, buf.shape[1]
        self.z_send, self.z_recv = sems.take(8), sems.take(8)
        self.x_send, self.x_recv, self.x_far = sems.take(2), [sems.take(8), sems.take(8)], sems.take(8)
        self.y_send, self.y_recv = sems.take(2), sems.take(2)
        self.z_copies = []

    def shard(self, xs, s):
        place = self.place
        start = place.yl * 512 + ((place.x + xs + 4) % 4) * 128 + ((place.z + s + 8) % 8) * 16
        return self.buf.at[rows_at(start, 16)]

    def to_y(self, ref, s):
        side = side_of(s)
        remote(ref, ref, self.y_send[side], self.y_recv[side], self.place.yoff(1 - 2 * side))

    def pass_on(self, s):
        ref, place = self.shard(0, s), self.place
        for way, sign in ((0, 1), (1, -1)):
            remote(ref, ref, self.x_send[way], self.x_recv[way][s % 8], place.xoff(sign))
        self.to_y(ref, s)

    def start(self):
        ref = self.shard(0, 0)
        for s in (1, -1, 2, -2, 3, -3, 4):
            self.z_copies.append(remote(ref, ref, self.z_send[s % 8], self.z_recv[-s % 8], self.place.zoff(s)))
        self.pass_on(0)

    def z_step(self, step):
        for s in sorted({-step, step} - {-4}):
            await_bytes(self.shard(0, s), self.z_recv[s % 8])
            self.pass_on(s)

    def x_step(self, step):
        for s in sorted({-step, step} - {-4}):
            for way, sign in ((0, 1), (1, -1)):
                ref = self.shard(-sign, s)
                await_bytes(ref, self.x_recv[way][s % 8])
                if side_of(s) == way:
                    remote(ref, ref, self.x_send[way], self.x_far[s % 8], self.place.xoff(sign))
                self.to_y(ref, s)

    def far_step(self, step):
        for s in sorted({-step, step} - {-4}):
            ref = self.shard(2, s)
            await_bytes(ref, self.x_far[s % 8])
            self.to_y(ref, s)

    def finish(self):
        for copy in self.z_copies:
            copy.wait_send()
        for side in range(2):
            await_bytes(self.buf.at[pl.ds(0, 256)], self.y_recv[side])
            await_bytes(self.buf.at[pl.ds(0, 192)], self.x_send[side])
            await_bytes(self.buf.at[pl.ds(0, 256)], self.y_send[side])


def add_rows(dst, start, count, *sources):
    @pl.loop(0, count // 32)
    def _(step):
        rows = rows_at(start + step * 32, 32)
        total = dst[rows, :].astype(jnp.float32)
        for ref, first in sources:
            total = total + ref[rows_at(first + step * 32, 32), :].astype(jnp.float32)
        dst[rows, :] = total.astype(dst.dtype)


class Scatter:
    def __init__(self, place, part, y_stage, x_stage, x_last, z_stage, sems):
        self.place, self.part, self.y_stage = place, part, y_stage
        self.x_stage, self.x_last, self.z_stage = x_stage, x_last, z_stage
        self.y_send, self.y_recv = sems.take(2), [sems.run(4), sems.run(4)]
        self.x_send, self.x_recv = sems.take(4), sems.take(4)
        self.z_send, self.z_recv = sems.run(8), sems.run(8)
        self.mine, self.other = place.yl * 512, (1 - place.yl) * 512

    def block(self, xs):
        return ((self.place.x + xs + 4) % 4) * 128

    def y_start(self):
        @pl.loop(0, 4)
        def _(index):
            start = self.block(jnp.where(index == 2, 3, jnp.where(index == 3, 0, 2 - index)))
            for side, sign in ((0, 1), (1, -1)):
                at = start + side * 64
                remote(
                    self.part.at[rows_at(self.other + at, 64)], self.y_stage.at[rows_at(at, 64)],
                    self.y_send[side], self.y_recv[side](index), self.place.yoff(sign),
                )

    def take_y(self, index, xs):
        start = self.block(xs)
        for side in range(2):
            await_bytes(self.y_stage.at[rows_at(start + side * 64, 64)], self.y_recv[side](index))
        add_rows(self.part, self.mine + start, 128, (self.y_stage, start))

    def x_one(self):
        for index, xs in enumerate((2, 1, -1)):
            self.take_y(index, xs)
            remote(self.part.at[rows_at(self.mine + self.block(xs), 128)], self.x_last.at[index],
                   self.x_send[index], self.x_recv[index], self.place.xoff(xs))

    def row(self, s):
        return rows_at(self.mine + self.block(0) + ((self.place.z + s) % 8) * 16, 16)

    def z_start(self):
        self.take_y(3, 0)
        for index in range(3):
            await_bytes(self.x_last.at[index], self.x_recv[index])
        add_rows(self.part, self.mine + self.block(0), 128, *[(self.x_last.at[index], 0) for index in range(3)])
        self.z_out()

    def z_out(self):
        @pl.loop(1, 8)
        def _(s):
            remote(self.part.at[self.row(s)], self.z_stage.at[s], self.z_send(s), self.z_recv(s), self.place.zoff(s))

    def z_drain(self):
        @pl.loop(1, 8)
        def _(s):
            await_bytes(self.part.at[pl.ds(0, 16)], self.z_send(s))

    def total(self):
        @pl.loop(1, 8)
        def _(s):
            await_bytes(self.z_stage.at[s], self.z_recv(s))

        total = self.part[self.row(0), :].astype(jnp.float32)
        for s in range(1, 8):
            total = total + self.z_stage[s].astype(jnp.float32)
        return total

    def finish(self):
        self.z_drain()
        for index in range(3):
            await_bytes(self.part.at[pl.ds(0, 128)], self.x_send[index])
        for side in range(2):
            await_bytes(self.part.at[pl.ds(0, 256)], self.y_send[side])


SEMS = 312
class ScatterX(Scatter):
    def x_one(self):
        for way, sign in ((0, 1), (1, -1)):
            remote(self.part.at[rows_at(way * 512 + self.block(2), 128)], self.x_stage.at[pl.ds(way * 128, 128)],
                   self.x_send[way], self.x_recv[way], self.place.xoff(sign))

    def x_two(self):
        for way, sign in ((0, 1), (1, -1)):
            await_bytes(self.x_stage.at[pl.ds(way * 128, 128)], self.x_recv[way])
            add_rows(self.part, way * 512 + self.block(sign), 128, (self.x_stage, way * 128))
            for yl in range(2):
                remote(self.part.at[rows_at(yl * 512 + self.block(sign), 128)],
                       self.x_last.at[way, pl.ds(yl * 128, 128)],
                       self.x_send[2 + way], self.x_recv[2 + way], self.place.xoff(sign))

    def y_start(self):
        for way in range(2):
            await_bytes(self.x_last.at[way], self.x_recv[2 + way])
        for yl in range(2):
            last = [(self.x_last.at[way], yl * 128) for way in range(2)]
            add_rows(self.part, yl * 512 + self.block(0), 128, *last)
        for side, sign in ((0, 1), (1, -1)):
            remote(self.part.at[rows_at(self.other + self.block(0) + side * 64, 64)],
                   self.y_stage.at[pl.ds(side * 64, 64)],
                   self.y_send[side], self.y_recv[side](0), self.place.yoff(sign))

    def z_start(self):
        for side in range(2):
            await_bytes(self.y_stage.at[pl.ds(side * 64, 64)], self.y_recv[side](0))
        add_rows(self.part, self.mine + self.block(0), 128, (self.y_stage, 0))
        self.z_out()

    def finish(self):
        self.z_drain()
        for way in range(2):
            await_bytes(self.part.at[pl.ds(0, 128)], self.x_send[way])
            await_bytes(self.part.at[pl.ds(0, 256)], self.x_send[2 + way])
            await_bytes(self.part.at[pl.ds(0, 64)], self.y_send[way])


GROUPS = ((0, 2), (1, 3))
LOCAL = [(0, p) for group in GROUPS for p in group] + [
    (sec, p) for group in GROUPS for sec in (1, 2) for p in group
]
PIECES = (
    [(3, p) for p in range(4)],
    [(sec, p) for sec in range(2) for p in GROUPS[0]],
    [(2, p) for p in GROUPS[0]],
    [(sec, p) for sec in range(2) for p in GROUPS[1]],
    [(2, p) for p in GROUPS[1]],
)
X_FIRST = (2, 4)


def spot(block):
    return (block % 2) * 4 + block // 2


def normed_of(wide):
    center = wide - jnp.mean(wide, axis=-1, keepdims=True)
    inverse = lax.rsqrt(jnp.mean(center * center, axis=-1, keepdims=True) + norm_eps)
    return center * inverse, inverse


def slope(delta):
    return delta * lax.rsqrt(delta * delta + smooth_width * smooth_width)


def head_masks():
    lane = lax.broadcasted_iota(jnp.int32, (64, 256), 1) // 64
    return [(lane == h).astype(jnp.float32) for h in range(4)]


def spread_heads(block, masks):
    wide = block.astype(jnp.float32)
    return jnp.concatenate([(wide * mask).astype(jnp.bfloat16) for mask in masks], axis=0)


def fold_heads(wide, masks):
    total = wide[0:64] * masks[0]
    for h in range(1, 4):
        total = total + wide[h * 64 : (h + 1) * 64] * masks[h]
    return total


def whole_kernel(
    factor, ens_hbm, target_hbm, win_hbm, wout_hbm, start_ref, end_ref, gin_ref, gwin_ref, gwout_ref,
    target_ref, win_ref, wout_ref,
    w_all, ens, nrm, nrm_t, q, kv, acc_q, acc_kv, mask, probs, att, att_t, outs, cot, cot_full,
    ga_part, ga_recv, ga, gq, own_kv, gkv, h_recv, gn, gn_recv, *rest,
):
    *stages, pair, sem_array = rest
    place = Place()
    sems = Sems(sem_array)
    c, yl = place.c, place.yl
    own = yl * 512 + place.x * 128 + place.z * 16
    bf16, f32 = jnp.bfloat16, jnp.float32
    place.signal()
    mine = rows_at(c * 128, 128)
    theirs = rows_at((1 - c) * 128, 128)
    loads = [
        pltpu.make_async_copy(src, dst, sems.take())
        for src, dst in (
            (win_hbm, win_ref), (wout_hbm, wout_ref), (ens_hbm, ens.at[1, mine]), (target_hbm, target_ref)
        )
    ]
    for load in loads:
        load.start()
    for load in loads[:2]:
        load.wait()
    for t, (sec, p) in enumerate(LOCAL):
        w_all[rows_at(own, 16), pl.ds(t * 128, 128)] = win_ref[:, lanes(sec * 1024 + c * 512 + p * 128, 128)]
    w_all[rows_at(own, 16), pl.ds(1536, 512)] = wout_ref[:, lanes(c * 512, 512)]
    loads[2].wait()

    def norm_rows(b, core):
        @pl.loop(0, 4)
        def _(step):
            rows = rows_at(core * 128 + step * 32, 32)
            normed = normed_of(ens[b, rows, :].astype(f32))[0].astype(bf16)
            for block in range(8):
                nrm[b, rows, pl.ds(spot(block) * 128, 128)] = normed[:, block * 128 : (block + 1) * 128]

    norm_rows(1, c)
    loads[3].wait()
    place.await_all()
    gi = Gather(place, w_all, sems)
    gi.start()
    ens_own = remote(ens.at[1, mine], ens.at[1, mine], sems.take(), sems.take(), place.sibling())
    position = place.goff(0)[1] * 64 - 64 + lax.broadcasted_iota(jnp.int32, (192, 256), 0)
    starts_here = jnp.concatenate([start_ref[...]] * 4, axis=1)
    ends_here = jnp.concatenate([end_ref[...]] * 4, axis=1)
    valid = (position >= starts_here) & (position < ends_here)
    mask[...] = valid.astype(f32)
    gi.z_step(1)
    gi.x_step(0)
    gi.z_step(2)
    gi.x_step(1)
    gi.far_step(0)
    gi.z_step(3)
    halo = [
        remote(ens.at[1, mine], ens.at[0, mine], sems.take(), sems.take(), place.goff(1)),
        remote(ens.at[1, mine], ens.at[2, mine], sems.take(), sems.take(), place.goff(-1)),
    ]
    gi.x_step(2)
    gi.far_step(1)
    ens_own.wait()
    norm_rows(1, 1 - c)
    gi.z_step(4)
    gi.x_step(3)
    gi.far_step(2)

    gi.x_step(4)
    gi.far_step(3)
    gi.far_step(4)
    half_one, half_two = lanes(yl * 512, 512), lanes((1 - yl) * 512, 512)

    def first_half(b):
        @pl.loop(0, 4)
        def _(j):
            acc_kv[b, :, lanes(j * 256, 256)] = dot(nrm[b, :, half_one], w_all[half_one, lanes(512 + j * 256, 256)], NN)

    first_half(1)

    @pl.loop(0, 2)
    def _(j):
        cols = lanes(j * 256, 256)
        acc_q[:, cols] = dot(nrm[1, :, half_one], w_all[half_one, cols], NN)

    for copy in halo:
        copy.wait_recv()
    onward = [
        remote(ens.at[b, mine], ens.at[b, mine], sems.take(), sems.take(), place.sibling()) for b in (0, 2)
    ]
    norm_rows(0, c)
    norm_rows(2, c)
    for copy in onward:
        copy.wait()
    for copy in halo:
        copy.wait_send()
    norm_rows(0, 1 - c)
    norm_rows(2, 1 - c)

    @pl.loop(0, 2)
    def _(t):
        first_half(2 * t)

    gi.finish()

    @pl.loop(0, 4)
    def _(j):
        cols = lanes(512 + j * 256, 256)
        to = lanes(j * 256, 256)
        for b in range(3):
            done = (acc_kv[b, :, to] + dot(nrm[b, :, half_two], w_all[half_two, cols], NN)).astype(bf16)
            for m in range(4):
                kv[m, pl.ds(b * 64, 64), to] = done[m * 64 : (m + 1) * 64]

    @pl.loop(0, 2)
    def _(j):
        cols = lanes(j * 256, 256)
        done = (acc_q[:, cols] + dot(nrm[1, :, half_two], w_all[half_two, cols], NN)).astype(bf16)
        q[:, cols] = (done.astype(f32) * 0.125).astype(bf16)

    masks = head_masks()
    att_send, att_recv = sems.run(8), sems.run(8)

    @pl.loop(0, 4)
    def _(m):
        rows = rows_at(m * 64, 64)
        for grp in range(2):
            cols = pl.ds(grp * 256, 256)
            q4 = spread_heads(q[rows, cols], masks)
            scores = dot(kv[m, :, pl.ds(grp * 512, 256)], q4, NT)
            scores = jnp.where(mask[...] > 0.5, scores, masked_score)
            raised = jnp.exp(scores - jnp.max(scores, axis=0, keepdims=True))
            weights = raised * (1.0 / jnp.sum(raised, axis=0, keepdims=True))
            probs[m * 2 + grp] = weights
            mixed = dot(weights.astype(bf16), kv[m, :, pl.ds(grp * 512 + 256, 256)], TN)
            to = lanes(grp * 512 + c * 256, 256)
            att[rows, to] = fold_heads(mixed, masks).astype(bf16)
            remote(att.at[rows, to], att.at[rows, to], att_send(m * 2 + grp), att_recv(m * 2 + grp), place.sibling())


    def await_att(sem, col):
        @pl.loop(0, 4)
        def _(m):
            for grp in range(2):
                await_bytes(att.at[rows_at(m * 64, 64), lanes(grp * 512 + col * 256, 256)], sem(m * 2 + grp))

    await_att(att_recv, 1 - c)
    out_send, out_recv = sems.run(2), sems.run(2)

    @pl.loop(0, 2)
    def _(j):
        cols = lanes(j * 256, 256)
        done = ens[1, :, lanes(c * 512 + j * 256, 256)].astype(f32) + dot(att[...], w_all[:, lanes(1536 + j * 256, 256)], NN)
        outs[0, :, cols] = done.astype(bf16)
        remote(outs.at[0, :, cols], outs.at[1, :, cols], out_send(j), out_recv(j), place.yoff(2))

    @pl.loop(0, 8)
    def _(j):
        rows = rows_at(j * 128, 128)
        cols = lanes(j * 128, 128)
        att_t[rows, :] = att[:, cols].T
        for b in range(3):
            nrm_t[rows, pl.ds(b * 256, 256)] = nrm[b, :, cols].T

    coef = (1.0 - (1.0 - fair_alpha) / 8) / 7
    @pl.loop(0, 2)
    def _(j):
        cols = lanes(j * 256, 256)
        await_bytes(outs.at[1, :, cols], out_recv(j))

        @pl.loop(0, 4)
        def _(step):
            row = step * 16
            near = [outs[0, rows_at(m * 64 + row, 16), cols].astype(f32) for m in range(4)]
            far = [outs[1, rows_at(m * 64 + row, 16), cols].astype(f32) for m in range(4)]
            target = target_ref[rows_at(row, 16), lanes(c * 512 + j * 256, 256)].astype(f32)
            spread = [None] * 4
            for m in range(4):
                for n in range(m + 1, 4):
                    term = slope(near[m] - near[n])
                    spread[m] = term if spread[m] is None else spread[m] + term
                    spread[n] = -term if spread[n] is None else spread[n] - term
            for m in range(4):
                for n in range(4):
                    spread[m] = spread[m] + slope(near[m] - far[n])
                cot[rows_at(m * 64 + row, 16), cols] = (slope(near[m] - target) - coef * spread[m]).astype(bf16)


    ga_out, ga_in = sems.run(2), sems.run(2)

    @pl.loop(0, 4)
    def _(t):
        grp = t % 2
        cols = lanes(grp * 256, 256)
        side = jnp.where(t < 2, 1 - c, c)
        part = dot(cot[...], w_all[rows_at(grp * 512 + side * 256, 256), pl.ds(1536, 512)], NT)
        ga_part[t // 2, :, cols] = part

        @pl.when(t < 2)
        def _():
            remote(ga_part.at[0, :, cols], ga_recv.at[:, cols], ga_out(grp), ga_in(grp), place.sibling())

    to = lanes(c * 512, 512)
    cot_full[:, to] = cot[mine, :]
    cot_copy = remote(cot.at[theirs], cot_full.at[:, to], sems.take(), sems.take(), place.sibling())

    @pl.loop(0, 2)
    def _(grp):
        cols = lanes(grp * 256, 256)
        await_bytes(ga_recv.at[:, cols], ga_in(grp))
        ga[:, cols] = (ga_part[1, :, cols] + ga_recv[:, cols]).astype(bf16)

    pieces = [
        (ScatterX if i in X_FIRST else Scatter)(place, *stages[i * 5 : i * 5 + 5], sems) for i in range(len(PIECES))
    ]
    so, s0, v0, sa, v1 = pieces
    other_rows, mine_rows = (1 - yl) * 512, yl * 512
    mid = pl.ds(256, 256)

    def outer(piece, first, terms, parts=2):
        @pl.loop(0, parts)
        def _(i):
            rows = rows_at(first + i * 256, 256)
            for t, (left, inner, right, start) in enumerate(terms):
                piece.part[rows, pl.ds(t * 256, 256)] = dot(
                    left[rows, inner], right[:, pl.ds(start, 256)], NN
                ).astype(bf16)

    every = pl.ds(0, 768)
    all_o = [(att_t, pl.ds(0, 256), cot, 0), (att_t, pl.ds(0, 256), cot, 256)]
    all_q = [(nrm_t, mid, gq, 0), (nrm_t, mid, gq, 256)]
    all_kv = [(nrm_t, every, gkv, t * 256) for t in range(4)]
    all_0 = [all_q[0], all_kv[0]]
    all_a = [all_q[1], all_kv[2]]
    outer(so, other_rows, all_o)
    so.y_start()
    halos = []

    def back(grp):
        cols = pl.ds(grp * 256, 256)
        kcols = pl.ds(grp * 512, 256)
        vcols = pl.ds(grp * 512 + 256, 256)

        @pl.loop(0, 4)
        def _(m):
            rows = rows_at(m * 64, 64)
            q4 = spread_heads(q[rows, cols], masks)
            g4 = spread_heads(ga[rows, cols], masks)
            keys = kv[m, :, kcols]
            weights = probs[m * 2 + grp]
            grad = dot(kv[m, :, vcols], g4, NT)
            inner = jnp.sum(weights * grad, axis=0, keepdims=True)
            grad_scores = (weights * (grad - inner)).astype(bf16)
            for at, value in (
                (vcols, dot(weights.astype(bf16), g4, NN)), (kcols, dot(grad_scores, q4, NN))
            ):
                own_kv[rows, at] = value[64:128]
                rounded = value.astype(bf16)
                for b in range(3):
                    gkv[rows_at(b * 256 + m * 64, 64), at] = rounded[b * 64 : (b + 1) * 64]
            gq[rows, cols] = (fold_heads(dot(grad_scores, keys, TN), masks) * 0.125).astype(bf16)

    def send_halo(grp):
        at = pl.ds(grp * 512, 512)
        halos.append(
            [
                remote(gkv.at[pl.ds(0, 256), at], h_recv.at[0, :, at], sems.take(), sems.take(), place.goff(-1)),
                remote(gkv.at[pl.ds(512, 256), at], h_recv.at[1, :, at], sems.take(), sems.take(), place.goff(1)),
            ]
        )

    back(0)
    send_halo(0)
    outer(s0, other_rows, all_0)
    s0.y_start()
    outer(so, mine_rows, all_o)
    so.x_one()
    outer(v0, 0, [all_kv[1]], 4)
    v0.x_one()
    back(1)
    send_halo(1)
    outer(sa, other_rows, all_a)
    sa.y_start()
    outer(v1, 0, [all_kv[3]], 4)
    v1.x_one()
    outer(s0, mine_rows, all_0)
    v0.x_two()
    so.z_start()
    outer(sa, mine_rows, all_a)
    s0.x_one()
    v1.x_two()
    @pl.loop(0, 4)
    def _(j):
        rows = rows_at(j * 256, 256)
        gn[:, lanes(j * 256, 256)] = dot(gq[...], w_all[rows, pl.ds(0, 512)], NT)

    pair_copies = {}
    starts = [0]
    for blocks in PIECES:
        starts.append(starts[-1] + len(blocks) * 128)

    def settle(i):
        at = pl.ds(starts[i], starts[i + 1] - starts[i])
        pair[0, :, at] = pieces[i].total().astype(bf16)
        pair_copies[i] = [
            remote(pair.at[0, :, at], pair.at[slot, :, at], sems.take(), sems.take(), device)
            for slot, device in ((3, place.far_sibling()), (1, place.yoff(2)), (2, place.sibling()))
        ]

    def deliver(i):
        for copy in pair_copies[i]:
            copy.wait_recv()
        for side, slot in ((c, 0), (1 - c, 2)):
            for t, (sec, p) in enumerate(PIECES[i]):
                at = pl.ds(starts[i] + t * 128, 128)
                value = (pair[slot, :, at].astype(f32) + pair[slot + 1, :, at].astype(f32)) * factor
                if sec == 3:
                    gwout_ref[:, lanes(side * 512 + p * 128, 128)] = value
                else:
                    gwin_ref[:, lanes(sec * 1024 + side * 512 + p * 128, 128)] = value

    v0.y_start()
    settle(0)
    sa.x_one()
    v1.y_start()
    s0.z_start()
    v0.z_start()
    for pair_halo in halos:
        for copy in pair_halo:
            copy.wait()
    for grp in range(2):
        @pl.loop(0, 4)
        def _(m):
            rows = rows_at(m * 64, 64)
            at = pl.ds(grp * 512, 512)
            gkv[rows_at(256 + m * 64, 64), at] = (
                own_kv[rows, at] + h_recv[0, rows, at].astype(f32) + h_recv[1, rows, at].astype(f32)
            ).astype(bf16)

    @pl.loop(0, 4)
    def _(j):
        rows = rows_at(j * 256, 256)
        cols = lanes(j * 256, 256)
        gn[:, cols] = gn[:, cols] + dot(gkv[pl.ds(256, 256), :], w_all[rows, pl.ds(512, 1024)], NT)

    gn_copy = remote(gn.at[theirs], gn_recv, sems.take(), sems.take(), place.sibling())
    v1.z_start()
    sa.z_start()
    settle(1)
    settle(2)
    deliver(0)
    gn_copy.wait_recv()
    cot_copy.wait_recv()

    @pl.loop(0, 8)
    def _(step):
        rows = rows_at(step * 16, 16)
        normed, inverse = normed_of(ens[1, rows_at(c * 128 + step * 16, 16), :].astype(f32))
        summed = gn[rows_at(c * 128 + step * 16, 16), :] + gn_recv[rows, :]
        grad = jnp.concatenate([summed[:, spot(b) * 128 : (spot(b) + 1) * 128] for b in range(8)], axis=1)
        first = jnp.mean(grad, axis=-1, keepdims=True)
        second = jnp.mean(grad * normed, axis=-1, keepdims=True)
        gin_ref[rows, :] = (
            cot_full[rows, :].astype(f32) + inverse * (grad - first - normed * second)
        ).astype(bf16)

    settle(4)
    settle(3)
    for i in (1, 2, 4, 3):
        deliver(i)
    for copy in [gn_copy, cot_copy] + sum(pair_copies.values(), []):
        copy.wait_send()
    for j in range(2):
        cols = pl.ds(j * 256, 256)
        await_bytes(outs.at[0, :, cols], out_send(j))
        await_bytes(ga_part.at[0, :, cols], ga_out(j))
    await_att(att_send, c)
    for piece in pieces:
        piece.finish()
    assert sems.used <= SEMS


def local(ensemble, target_field, weight_in, weight_out, window_start, window_end):
    mem_dev, points, width = ensemble.shape
    bf16, f32 = jnp.bfloat16, jnp.float32
    count = mem_dev * lax.axis_size("member") * points * lax.axis_size("grid")
    vmem = pl.BlockSpec(memory_space=pltpu.VMEM)
    stages = [
        pltpu.VMEM(shape + (len(blocks) * 128,), bf16)
        for i, blocks in enumerate(PIECES)
        for shape in (
            ((1024,), (128,), (256,), (2, 256), (8, 16)) if i in X_FIRST else ((1024,), (512,), (16,), (3, 128), (8, 16))
        )
    ]

    grad_input, grad_in, grad_out = pl.pallas_call(
        functools.partial(whole_kernel, 1.0 / math.sqrt(count)),
        name="k_whole",
        out_shape=[
            jax.ShapeDtypeStruct((mem_dev * points, width), bf16),
            jax.ShapeDtypeStruct(weight_in.shape, f32),
            jax.ShapeDtypeStruct(weight_out.shape, f32),
        ],
        in_specs=[pl.BlockSpec(memory_space=pl.ANY)] * 4 + [vmem] * 2,
        out_specs=[vmem] * 3,
        scratch_shapes=[
            pltpu.VMEM((points, width), bf16),
            pltpu.VMEM((16, 3072), bf16),
            pltpu.VMEM((16, 1024), bf16),
            pltpu.VMEM((1024, 2048), bf16),
            pltpu.VMEM((3, 256, 1024), bf16),
            pltpu.VMEM((3, 256, 1024), bf16),
            pltpu.VMEM((1024, 768), bf16),
            pltpu.VMEM((256, 512), bf16),
            pltpu.VMEM((4, 192, 1024), bf16),
            pltpu.VMEM((256, 512), f32),
            pltpu.VMEM((3, 256, 1024), f32),
            pltpu.VMEM((192, 256), f32),
            pltpu.VMEM((8, 192, 256), f32),
            pltpu.VMEM((256, 1024), bf16),
            pltpu.VMEM((1024, 256), bf16),
            pltpu.VMEM((2, 256, 512), bf16),
            pltpu.VMEM((256, 512), bf16),
            pltpu.VMEM((128, 1024), bf16),
            pltpu.VMEM((2, 256, 512), f32),
            pltpu.VMEM((256, 512), f32),
            pltpu.VMEM((256, 512), bf16),
            pltpu.VMEM((256, 512), bf16),
            pltpu.VMEM((256, 1024), f32),
            pltpu.VMEM((768, 1024), bf16),
            pltpu.VMEM((2, 256, 1024), bf16),
            pltpu.VMEM((256, 1024), f32),
            pltpu.VMEM((128, 1024), f32),
        ]
        + stages
        + [
            pltpu.VMEM((4, 16, 2048), bf16),
            pltpu.SemaphoreType.DMA((SEMS,)),
        ],
        compiler_params=pltpu.CompilerParams(
            collective_id=1, has_side_effects=True, vmem_limit_bytes=56 << 20
        ),
    )(ensemble.reshape(mem_dev * points, width), target_field, weight_in, weight_out,
      window_start.reshape(1, points), window_end.reshape(1, points))
    return grad_input.reshape(ensemble.shape), grad_in, grad_out


norm_eps = 1e-05
smooth_width = 0.1
fair_alpha = 0.95
masked_score = -1e30


def solution(mesh):
    in_specs = (
        P("member", "grid", None),
        P("grid", None),
        P("grid", None),
        P("grid", None),
        P("grid"),
        P("grid"),
    )
    out_specs = (P("member", "grid", None), P("grid", None), P("grid", None))
    return jax.shard_map(local, mesh=mesh, in_specs=in_specs, out_specs=out_specs, check_vma=False)
```
